512 devices in a mesh: branch: 128 (over x, z, core), sub: 4 (over y).
Axes of the slice: x: 4, y: 4, z: 16, core: 2. Of those that a mesh axis runs over, the one named last changes fastest.
Arguments:
- rhs: bfloat16 [16, 2097152], P(None, ('branch', 'sub')), may hold values from -6 to 6
- coords: bfloat16 [3, 2097152], P(None, ('branch', 'sub')), may hold values from 0 to 1, as said below
- basis: bfloat16 [8192, 64, 256], P(('branch', 'sub')), may hold values from -0.375 to 0.375
- leaf_transfer: bfloat16 [8192, 64, 64], P(('branch', 'sub')), may hold values from -0.1875 to 0.1875
- device_transfer: bfloat16 [512, 64, 64], P(('branch', 'sub')), may hold values from -0.375 to 0.375
- transfer_one: bfloat16 [128, 64, 64], replicated, may hold values from -0.5 to 0.5
- transfer_two: bfloat16 [64, 64, 64], replicated, may hold values from -0.5 to 0.5
- transfer_three: bfloat16 [32, 64, 64], replicated, may hold values from -0.5 to 0.5
- far_list: int32 [512, 16], P(('branch', 'sub')), may hold values from 0 to 511, as said below
- far_count: int32 [512], P(('branch', 'sub')), may hold values from 1 to 16, as said below
- far_coupling: bfloat16 [512, 16, 64, 64], P(('branch', 'sub')), may hold values from -1.796875 to 1.796875
- top_list: int32 [128, 4, 8], P('branch'), may hold values from 0 to 127, as said below
- top_coupling: bfloat16 [128, 4, 8, 64, 64], P('branch'), may hold values from -1.796875 to 1.796875
- near_list: int32 [8192, 8], P(('branch', 'sub')), may hold values from 0 to 8191, as said below
Outputs:
- result: float32 [16, 2097152], P(None, ('branch', 'sub'))
The draws below stay inside these ranges and needn't reach their ends.
Inputs may be any that keep to these rules, and one draw needn't show every extreme that they name: `coords`: each leaf's points lie in and around that leaf's own cell of a grid of 8192 cells in the unit cube; consecutive leaves have nearby cells. `near_list`: row i starts with i itself; the other entries are distinct leaves of the cluster i // 16 or of the clusters just before and after it in the order branch, then sub. `far_list`: the entries of a row are distinct and differ from the row's own cluster; only the first far_count slots are read. `far_count`: some cluster uses all 16 slots. `top_list`: entry [b, l, j] names a node of level l + 1, so it is below 128 // 2**l.
All inputs are finite; a program needn't handle non-finite values.
Results may differ from the reference program's by a relative error of at most 0.0029.
Values may be sent and summed in bfloat16 or wider, within the bound.
No kernel may reach another device: no remote copies, remote signals or barrier semaphores. Data moves between devices by JAX's collectives and lax.ppermute only.
A program may use at most 64 MiB of HBM per device.

```python
import jax
import jax.numpy as jnp
from jax import lax

RANK = 64
RHS_COLS = 16
LEAF_SIZE = 256
LEAF_DEV = 16
NEAR_SLOTS = 8
FAR_SLOTS = 16
TOP_SLOTS = 8
BRANCHES = 128
SUBS = 4
CLUSTERS = 512
LEAVES = 8192
POINTS = 2097152


def cell_corner(leaf_ids, total_bits, axis_slot):
    place = jnp.zeros_like(leaf_ids)
    for level in range(8):
        source_bit = 3 * level + axis_slot
        if source_bit < total_bits:
            place = place + (leaf_ids >> source_bit & 1) * 2 ** level
    return place


def draw_coords(key, part):
    key = jax.random.fold_in(key, 15)
    total_bits = LEAVES.bit_length() - 1
    leaf_ids = (jnp.arange(POINTS, dtype=jnp.int32) // LEAF_SIZE).astype(jnp.int32)
    offsets = jax.random.uniform(key, (3, POINTS), jnp.float32)
    rows = []
    for axis_slot in range(3):
        axis_bits = (total_bits + 2 - axis_slot) // 3
        cells = 2 ** axis_bits
        corner = cell_corner(leaf_ids, total_bits, axis_slot).astype(jnp.float32)
        spot = (corner + 0.5 + 1.5 * (offsets[axis_slot] - 0.5)) / cells
        rows.append(jnp.clip(spot, 0.0, 1.0))
    return jnp.stack(rows).astype(jnp.bfloat16)


def draw_near_list(key, part):
    key = jax.random.fold_in(key, 11)
    leaf_ids = jnp.arange(LEAVES, dtype=jnp.int32)
    owners = leaf_ids // LEAF_DEV
    window = 3 * LEAF_DEV
    shuffled = jax.vmap(lambda row_key: jax.random.permutation(row_key, window))(jax.random.split(key, LEAVES))
    candidates = (owners[:, None] - 1) * LEAF_DEV + shuffled.astype(jnp.int32)
    usable = (candidates >= 0) & (candidates < LEAVES) & (candidates != leaf_ids[:, None])
    ranking = jnp.where(usable, 0, window) + jnp.arange(window, dtype=jnp.int32)[None, :]
    ordering = jnp.argsort(ranking, axis=1)
    chosen = jnp.take_along_axis(candidates, ordering[:, :NEAR_SLOTS - 1], axis=1)
    return jnp.concatenate([leaf_ids[:, None], chosen], axis=1).astype(jnp.int32)


def draw_far_list(key, part):
    key = jax.random.fold_in(key, 12)
    shuffled = jax.vmap(lambda row_key: jax.random.permutation(row_key, CLUSTERS - 1))(jax.random.split(key, CLUSTERS))
    offsets = 1 + shuffled[:, :FAR_SLOTS].astype(jnp.int32)
    return ((jnp.arange(CLUSTERS, dtype=jnp.int32)[:, None] + offsets) % CLUSTERS).astype(jnp.int32)


def draw_far_count(key, part):
    key = jax.random.fold_in(key, 13)
    count_key, slot_key = jax.random.split(key)
    counts = jax.random.randint(count_key, (CLUSTERS,), 1, FAR_SLOTS + 1)
    busiest = jax.random.randint(slot_key, (), 0, CLUSTERS)
    return jnp.where(jnp.arange(CLUSTERS) == busiest, FAR_SLOTS, counts).astype(jnp.int32)


def draw_top_list(key, part):
    key = jax.random.fold_in(key, 14)
    limits = (BRANCHES // jnp.array([1, 2, 4, 8], dtype=jnp.int32))[None, :, None]
    sampled = jax.random.randint(key, (BRANCHES, 4, TOP_SLOTS), 0, limits)
    rotated = (jnp.arange(BRANCHES, dtype=jnp.int32) + BRANCHES // 2) % BRANCHES
    sampled = sampled.at[:, 0, 0].set(rotated)
    return sampled.astype(jnp.int32)


def shard_levels(own_key, shape, pieces, low, top_value):
    factor_of, own = 1.0, jax.random.fold_in(own_key, 6)
    for dim, blocks in pieces:
        draws = jnp.exp(jax.random.uniform(jax.random.fold_in(own, dim), (blocks,), jnp.float32, low / len(pieces), top_value / len(pieces)))
        factor_of = factor_of * jnp.repeat(draws, shape[dim] // blocks).reshape([-1 if axis == dim else 1 for axis in range(len(shape))])
    return factor_of


def scatter_about(own_key, extent, scale, reach, cuts=(), held_as=jnp.bfloat16):
    gain = shard_levels(own_key, extent, cuts, -0.22, 0.18) if cuts else 1.0
    result = jax.random.normal(own_key, extent, jnp.float32) * scale * gain
    return jnp.minimum(jnp.maximum(result, -reach), reach).astype(held_as)


def setup_inputs(seed: int = 0) -> dict:
    streams_of = jax.random.split(jax.random.key(seed), 15)
    rhs = scatter_about(streams_of[0], (RHS_COLS, POINTS), 1.0, 6.0, ((1, 512),))
    coords = draw_coords(jax.random.fold_in(streams_of[14], 71), 0)
    basis = scatter_about(streams_of[2], (LEAVES, RANK, LEAF_SIZE), LEAF_SIZE ** -0.5, 0.375, ((0, 512),))
    leaf_transfer = scatter_about(streams_of[3], (LEAVES, RANK, RANK), (RANK * LEAF_DEV) ** -0.5, 0.1875, ((0, 512),))
    device_transfer = scatter_about(streams_of[4], (CLUSTERS, RANK, RANK), (RANK * SUBS) ** -0.5, 0.375, ((0, 512),))
    transfer_one = scatter_about(streams_of[5], (BRANCHES, RANK, RANK), (2 * RANK) ** -0.5, 0.5)
    transfer_two = scatter_about(streams_of[6], (BRANCHES // 2, RANK, RANK), (2 * RANK) ** -0.5, 0.5)
    transfer_three = scatter_about(streams_of[7], (BRANCHES // 4, RANK, RANK), (2 * RANK) ** -0.5, 0.5)
    far_list = draw_far_list(jax.random.fold_in(streams_of[14], 71), 0)
    far_count = draw_far_count(jax.random.fold_in(streams_of[14], 71), 0)
    far_coupling = scatter_about(streams_of[10], (CLUSTERS, FAR_SLOTS, RANK, RANK), 0.3, 1.796875, ((0, 512),))
    top_list = draw_top_list(jax.random.fold_in(streams_of[14], 71), 0)
    top_coupling = scatter_about(streams_of[12], (BRANCHES, 4, TOP_SLOTS, RANK, RANK), 0.3, 1.796875, ((0, 128),))
    near_list = draw_near_list(jax.random.fold_in(streams_of[14], 71), 0)
    return dict(rhs=rhs, coords=coords, basis=basis, leaf_transfer=leaf_transfer, device_transfer=device_transfer, transfer_one=transfer_one, transfer_two=transfer_two, transfer_three=transfer_three, far_list=far_list, far_count=far_count, far_coupling=far_coupling, top_list=top_list, top_coupling=top_coupling, near_list=near_list)


INV_LENGTH = 20.0
PRECISE = lax.Precision.HIGHEST

def kernel_tile(target_xyz, source_xyz):
    spread_xyz = target_xyz[:, None, :, None] - source_xyz[:, :, None, :]
    squared = lax.optimization_barrier(jnp.sum(spread_xyz * spread_xyz, axis=0))
    return jnp.exp(-INV_LENGTH * jnp.sqrt(squared)).astype(jnp.bfloat16)

def reference(rhs, coords, basis, leaf_transfer, device_transfer, transfer_one, transfer_two, transfer_three, far_list, far_count, far_coupling, top_list, top_coupling, near_list):
    rhs_blocks = rhs.reshape(RHS_COLS, LEAVES, LEAF_SIZE)
    xyz_blocks = coords.astype(jnp.float32).reshape(3, LEAVES, LEAF_SIZE)

    def per_cluster(operands):
        basis_here, rhs_here, transfer_here = operands
        leaf_coeffs = jnp.einsum('lkp,rlp->lkr', basis_here.astype(jnp.float32), rhs_here.astype(jnp.float32))
        return jnp.einsum('lij,ljr->ir', transfer_here.astype(jnp.float32), leaf_coeffs, precision=PRECISE)
    cluster_rhs = jnp.transpose(rhs_blocks.reshape(RHS_COLS, CLUSTERS, LEAF_DEV, LEAF_SIZE), (1, 0, 2, 3))
    coarse = lax.map(per_cluster, (basis.reshape(CLUSTERS, LEAF_DEV, RANK, LEAF_SIZE), cluster_rhs, leaf_transfer.reshape(CLUSTERS, LEAF_DEV, RANK, RANK)))
    lifted = jnp.einsum('dij,djr->dir', device_transfer.astype(jnp.float32), coarse, precision=PRECISE)
    level_one = lax.optimization_barrier(jnp.sum(lifted.reshape(BRANCHES, SUBS, RANK, RHS_COLS), axis=1))

    def pair_up(child, transfer):
        raised = jnp.einsum('nij,njr->nir', transfer.astype(jnp.float32), child, precision=PRECISE)
        return lax.optimization_barrier(jnp.sum(raised.reshape(-1, 2, RANK, RHS_COLS), axis=1))
    level_two = pair_up(level_one, transfer_one)
    level_three = pair_up(level_two, transfer_two)
    level_four = pair_up(level_three, transfer_three)
    far_sources = coarse[far_list]
    far_terms = jnp.einsum('djik,djkr->djir', far_coupling.astype(jnp.float32), far_sources, precision=PRECISE)
    live_mask = (jnp.arange(FAR_SLOTS)[None, :] < far_count[:, None]).astype(jnp.float32)
    device_far = lax.optimization_barrier(jnp.sum(far_terms * live_mask[:, :, None, None], axis=1))
    levels = (level_one, level_two, level_three, level_four)
    group_sums = []
    for level in range(4):
        picked = levels[level][top_list[:, level]]
        partial_terms = jnp.einsum('bjik,bjkr->bir', top_coupling[:, level].astype(jnp.float32), picked, precision=PRECISE)
        group_width = 2 ** level
        group_sums.append(lax.optimization_barrier(jnp.sum(partial_terms.reshape(BRANCHES // group_width, group_width, RANK, RHS_COLS), axis=1)))

    def lower(parent, transfer, fanout):
        return jnp.einsum('nij,nir->njr', transfer.astype(jnp.float32), jnp.repeat(parent, fanout, axis=0), precision=PRECISE)
    down_four = group_sums[3]
    down_three = group_sums[2] + lower(down_four, transfer_three, 2)
    down_two = group_sums[1] + lower(down_three, transfer_two, 2)
    down_one = group_sums[0] + lower(down_two, transfer_one, 2)
    down_zero = device_far + lower(down_one, device_transfer, SUBS)

    def near_leaf(operands):
        sources, target_index = operands
        source_rhs = rhs_blocks[:, sources]
        tile_vals = kernel_tile(xyz_blocks[:, target_index], xyz_blocks[:, sources])
        return jnp.einsum('rjq,jpq->rp', source_rhs.astype(jnp.float32), tile_vals.astype(jnp.float32))

    def finish(operands):
        basis_here, transfer_here, coarse_down, near_here, leaf_here = operands
        leaf_down = jnp.einsum('lij,ir->ljr', transfer_here.astype(jnp.float32), coarse_down, precision=PRECISE).astype(jnp.bfloat16)
        far_part = jnp.einsum('lkp,lkr->lrp', basis_here.astype(jnp.float32), leaf_down.astype(jnp.float32))
        near_part = jax.vmap(lambda sources, target_index: near_leaf((sources, target_index)))(near_here, leaf_here)
        return near_part + far_part
    leaf_ids = jnp.arange(LEAVES, dtype=jnp.int32).reshape(CLUSTERS, LEAF_DEV)
    blocks = lax.map(finish, (basis.reshape(CLUSTERS, LEAF_DEV, RANK, LEAF_SIZE), leaf_transfer.reshape(CLUSTERS, LEAF_DEV, RANK, RANK), down_zero, near_list.reshape(CLUSTERS, LEAF_DEV, NEAR_SLOTS), leaf_ids))
    return jnp.transpose(blocks, (2, 0, 1, 3)).reshape(RHS_COLS, POINTS)
```

```python
import functools

import jax
import jax.numpy as jnp
import numpy as np
from jax import lax
from jax.experimental import pallas as pl
from jax.experimental.pallas import tpu as pltpu
from jax.sharding import Mesh, PartitionSpec as P

F32 = jnp.float32
BF16 = jnp.bfloat16
DEV = ("x", "zh", "zl", "core", "y")
SCALE = float(20.0 * np.log2(np.e))
NT = (((1,), (1,)), ((), ()))
NN = (((1,), (0,)), ((), ()))
GRANT = 60 * 1024 * 1024
PACKED = 10240
ROOM = 98304


def dot(a, b, dims):
    return lax.dot_general(a, b, dims, preferred_element_type=F32)


def split(v):
    hi = v.astype(BF16)
    lo = (v - hi.astype(F32)).astype(BF16)
    return hi, lo


def wide_dot(v, b, dims):
    rows = v.shape[0]
    hi, lo = split(v)
    out = dot(jnp.concatenate([hi, lo], axis=0), b, dims)
    return out[:rows] + out[rows:]


def vmem(n):
    return [pl.BlockSpec(memory_space=pltpu.VMEM)] * n


def hbm(n):
    return [pl.BlockSpec(memory_space=pltpu.HBM)] * n


def smem(n):
    return [pl.BlockSpec(memory_space=pltpu.SMEM)] * n


def copies(sources, targets, sems):
    return [
        pltpu.make_async_copy(source, target, sems.at[k])
        for k, (source, target) in enumerate(zip(sources, targets))
    ]


def up_kernel(
    id_ref, rhs_hbm, coords_hbm, basis_hbm, lt_hbm, dt_hbm,
    out_ref, own_ref, rhs_ref, coords_ref, basis_ref, lt_ref, dt_ref, sems,
):
    moves = copies(
        (rhs_hbm, coords_hbm, basis_hbm, lt_hbm, dt_hbm),
        (rhs_ref, coords_ref, basis_ref, lt_ref, dt_ref),
        sems,
    )
    for move in moves:
        move.start()
    for move in moves:
        move.wait()
    total = jnp.zeros((16, 64), F32)
    for leaf in range(16):
        coeffs = dot(rhs_ref[:, leaf * 256 : (leaf + 1) * 256], basis_ref[leaf], NT)
        total = total + wide_dot(coeffs, lt_ref[leaf], NT)
    lifted = wide_dot(total, dt_ref[0], NT)
    even = (id_ref[0] >> 2) & 1 == 0
    first = jnp.where(even, lifted, total)
    second = jnp.where(even, total, lifted)
    both = jnp.concatenate([first, second], axis=1).astype(BF16)
    for k in range(16):
        out_ref[k] = both
    own_ref[0:16, :] = rhs_ref[...]
    xyz = coords_ref[...].astype(F32)
    own_ref[16:24, :] = jnp.concatenate([xyz, jnp.zeros((5, 4096), F32)], axis=0).astype(BF16)


def up_pass(dev, rhs, coords, basis, lt, dt):
    return pl.pallas_call(
        up_kernel,
        out_shape=[
            jax.ShapeDtypeStruct((16, 16, 128), BF16),
            jax.ShapeDtypeStruct((24, 4096), BF16),
        ],
        in_specs=smem(1) + hbm(5),
        out_specs=vmem(2),
        scratch_shapes=[
            pltpu.VMEM((16, 4096), BF16),
            pltpu.VMEM((3, 4096), BF16),
            pltpu.VMEM((16, 64, 256), BF16),
            pltpu.VMEM((16, 64, 64), BF16),
            pltpu.VMEM((1, 64, 64), BF16),
            pltpu.SemaphoreType.DMA((5,)),
        ],
        compiler_params=pltpu.CompilerParams(vmem_limit_bytes=GRANT),
        cost_estimate=pl.CostEstimate(flops=20_000_000, bytes_accessed=1_000_000, transcendentals=0),
        name="up_pass",
    )(dev, rhs, coords, basis, lt, dt)


def prepare(
    id_ref, t1_ref, t2_ref, t3_ref, fc_ref, tc_ref, packed_ref, path_ref
):
    def put(at, first, second):
        packed_ref[at * 64 : (at + 1) * 64, :] = jnp.concatenate([first, second], axis=1)

    for source, offset, nodes in ((t1_ref, 0, 64), (t2_ref, 64, 32), (t3_ref, 96, 16)):
        for n in range(nodes):
            put(offset + n, source[2 * n], source[2 * n + 1])
    for slot in range(16):
        put(112 + slot, fc_ref[0, slot], fc_ref[0, slot])
    for level in range(4):
        for slot in range(8):
            put(128 + level * 8 + slot, tc_ref[0, level, slot], tc_ref[0, level, slot])
    branch = id_ref[0] >> 2
    path_ref[0] = t1_ref[branch]
    path_ref[1] = t2_ref[branch >> 1]
    path_ref[2] = t3_ref[branch >> 2]


def features(xyz, centre):
    moved = (xyz - centre) * SCALE
    hi, lo = split(moved)
    exact = hi.astype(F32) + lo.astype(F32)
    norm = jnp.sum(exact * exact, axis=0, keepdims=True)
    n1 = norm.astype(BF16).astype(F32)
    n2 = (norm - n1).astype(BF16).astype(F32)
    n3 = norm - n1 - n2
    row = lax.broadcasted_iota(jnp.int32, xyz.shape, 0)
    norms = jnp.where(row == 0, n1, jnp.where(row == 1, n2, jnp.where(row == 2, n3, 0.0)))
    ones = jnp.where(row < 3, 1.0, 0.0)
    return hi.astype(F32), lo.astype(F32), norms, ones


def near_kernel(
    first, last, id_ref, near_ref, swap_a_ref, own_ref, swap_b_ref, out_ref, feat, rhs, target
):
    own_xyz = own_ref[16:24, :].astype(F32)
    low = jnp.min(own_xyz, axis=1, keepdims=True)
    high = jnp.max(own_xyz, axis=1, keepdims=True)
    centre = 0.5 * (low + high)
    for part, ref in enumerate((swap_a_ref, own_ref, swap_b_ref)):
        cols = pl.ds(part * 4096, 4096)
        rhs[:, cols] = ref[0:16, :]
        xyz = ref[16:24, :].astype(F32)
        hi, lo, norms, ones = features(xyz, centre)
        both = jnp.concatenate([hi, lo], axis=0).astype(BF16)
        feat[0:16, cols] = both
        feat[16:32, cols] = both
        feat[32:48, cols] = jnp.concatenate([ones, norms], axis=0).astype(BF16)
        if part == 1:
            for leaf in range(first, last):
                c = slice(leaf * 256, (leaf + 1) * 256)
                h = -2.0 * hi[:, c]
                m = -2.0 * lo[:, c]
                stack = jnp.concatenate([h, h, m, m, norms[:, c], ones[:, c]], axis=0)
                target[leaf - first] = jnp.transpose(stack).astype(BF16)
    base = (id_ref[0] - 1) * 16
    even = (id_ref[0] & 1) == 0

    def leaf_step(step, carry):
        left = target[step]
        total = jnp.zeros((16, 256), F32)
        for slot in range(8):
            source = near_ref[slot, first + step] - base
            source = jnp.minimum(jnp.maximum(source, 0), 47)
            part = source >> 4
            source = jnp.where(even, 2 - part, part) * 16 + (source & 15)
            cols = pl.ds(pl.multiple_of(source * 256, 256), 256)
            squared = jnp.maximum(dot(left, feat[:, cols], NN), 1e-20)
            tile = jnp.exp2(-(squared * lax.rsqrt(squared))).astype(BF16)
            total = total + dot(rhs[:, cols], tile, NT)
        out_ref[:, pl.ds(pl.multiple_of(step * 256, 256), 256)] = total
        return carry

    lax.fori_loop(0, last - first, leaf_step, 0, unroll=4)


def prep_kernel(
    id_ref, t1_hbm, t2_hbm, t3_hbm, fc_hbm, tc_hbm, packed_hbm, path_ref,
    packed, t1_ref, t2_ref, t3_ref, fc_ref, tc_ref, sems,
):
    moves = copies((t1_hbm, t2_hbm, t3_hbm, fc_hbm, tc_hbm), (t1_ref, t2_ref, t3_ref, fc_ref, tc_ref), sems)
    for move in moves:
        move.start()
    for move in moves:
        move.wait()
    prepare(id_ref, t1_ref, t2_ref, t3_ref, fc_ref, tc_ref, packed, path_ref)
    out = pltpu.make_async_copy(packed, packed_hbm.at[0:PACKED, :], sems.at[5])
    out.start()
    out.wait()


def prep_pass(dev, t1, t2, t3, fc, tc):
    return pl.pallas_call(
        prep_kernel,
        out_shape=[
            jax.ShapeDtypeStruct((ROOM, 128), BF16),
            jax.ShapeDtypeStruct((3, 64, 64), BF16),
        ],
        in_specs=smem(1) + hbm(5),
        out_specs=hbm(1) + vmem(1),
        scratch_shapes=[
            pltpu.VMEM((PACKED, 128), BF16),
            pltpu.VMEM((128, 64, 64), BF16),
            pltpu.VMEM((64, 64, 64), BF16),
            pltpu.VMEM((32, 64, 64), BF16),
            pltpu.VMEM((1, 16, 64, 64), BF16),
            pltpu.VMEM((1, 4, 8, 64, 64), BF16),
            pltpu.SemaphoreType.DMA((6,)),
        ],
        compiler_params=pltpu.CompilerParams(vmem_limit_bytes=GRANT),
        cost_estimate=pl.CostEstimate(flops=1_000_000, bytes_accessed=8_000_000, transcendentals=0),
        name="prep_pass",
    )(dev, t1, t2, t3, fc, tc)


def near_cost(leaves):
    return pl.CostEstimate(
        flops=400_000_000 * leaves, bytes_accessed=600_000, transcendentals=1_050_000 * leaves
    )


def near_scratch(leaves):
    return [
        pltpu.VMEM((48, 12288), BF16),
        pltpu.VMEM((16, 12288), BF16),
        pltpu.VMEM((leaves, 256, 48), BF16),
    ]


def near_field(dev, near_list, swap_a, own, swap_b, first, last):
    return pl.pallas_call(
        functools.partial(near_kernel, first, last),
        out_shape=jax.ShapeDtypeStruct((16, (last - first) * 256), F32),
        in_specs=smem(2) + vmem(3),
        out_specs=vmem(1)[0],
        scratch_shapes=near_scratch(last - first),
        compiler_params=pltpu.CompilerParams(vmem_limit_bytes=GRANT),
        cost_estimate=near_cost(last - first + 1),
        name="near_field",
    )(dev, near_list, swap_a, own, swap_b)


def mid_kernel(
    id_ref, flist_ref, fcount_ref, tlist_ref, own_ref, other_ref, packed_hbm,
    out_ref, shares_ref, nodes, packed, sem,
):
    move = pltpu.make_async_copy(packed_hbm.at[0:PACKED, :], packed, sem)
    move.start()
    my_core = (id_ref[0] >> 2) & 1
    lane16 = lax.broadcasted_iota(jnp.int32, (16, 128), 1)
    low16 = lane16 < 64
    half16 = jnp.where(low16, 0, 1)
    from_own = half16 == my_core

    def put(at, value):
        hi, lo = split(value)
        nodes[at] = jnp.concatenate([hi, lo], axis=0)

    def raise_four(pairs, weights):
        value = jnp.concatenate(pairs, axis=0)
        hi, lo = split(value)
        out = dot(jnp.concatenate([hi, lo], axis=0), weights, NT)
        out = out[:64] + out[64:]
        first = jnp.where(low16, out[0:16, 0:128], out[16:32, 0:128])
        second = jnp.where(low16, out[32:48, 128:256], out[48:64, 128:256])
        return first, second

    def side_by_side(first, count):
        return jnp.concatenate([packed[(first + k) * 64 : (first + k + 1) * 64, :] for k in range(count)], axis=1)

    ones = []
    for at_x in range(4):
        for z in range(16):
            at = (at_x * 64 + z) * 16
            sums = []
            for half in (own_ref, other_ref):
                parts = [half[y * 256 + at : y * 256 + at + 16, :].astype(F32) for y in range(4)]
                sums.append((parts[0] + parts[1]) + (parts[2] + parts[3]))
            ones.append(jnp.where(from_own, sums[0], sums[1]))
            put(at_x * 16 + z, ones[-1])
    move.wait()
    for at_x in range(4):
        twos = []
        for quad in range(4):
            node = at_x * 16 + quad * 4
            twos.extend(raise_four(ones[node : node + 4], packed[node * 64 : node * 64 + 256, :]))
        for k in range(8):
            put(64 + at_x * 8 + k, twos[k])
        threes = []
        for quad in range(2):
            row = (64 + at_x * 8 + quad * 4) * 64
            threes.extend(raise_four(twos[quad * 4 : quad * 4 + 4], packed[row : row + 256, :]))
        for k in range(4):
            put(96 + at_x * 4 + k, threes[k])
        row = (96 + at_x * 4) * 64
        fours = raise_four(threes, packed[row : row + 256, :])
        for k in range(2):
            put(112 + at_x * 2 + k, fours[k])

    blocks = []
    for slot in range(16):
        c = flist_ref[0, slot]
        c_y, c_core = c & 3, (c >> 2) & 1
        place = pl.multiple_of((((c >> 7) * 4 + c_y) * 16 + ((c >> 3) & 15)) * 16, 16)
        block = jnp.where(c_core == my_core, own_ref[pl.ds(place, 16), :], other_ref[pl.ds(place, 16), :])
        live = jnp.where(slot < fcount_ref[0], 1 - c_core, 2)
        blocks.append(block * jnp.where(half16 == live, 1.0, 0.0).astype(BF16))
    out_ref[16:32, :] = dot(jnp.concatenate(blocks, axis=1), side_by_side(112, 16), NT)

    parts = []
    for level, offset in enumerate((0, 64, 96, 112)):
        blocks = []
        for slot in range(8):
            node = tlist_ref[0, level, slot]
            block = nodes[offset + (node >> 1)]
            mask = jnp.where(half16 == (node & 1), 1.0, 0.0).astype(BF16)
            blocks.append(block * jnp.concatenate([mask, mask], axis=0))
        out = dot(jnp.concatenate(blocks, axis=1), side_by_side(128 + level * 8, 8), NT)
        parts.append(out[:16] + out[16:])
    out_ref[0:16, :] = parts[0]
    upper = jnp.concatenate([parts[1], parts[2]], axis=1)
    last = jnp.concatenate([parts[3], parts[3]], axis=1)
    for k in range(8):
        shares_ref[k, 0:16, :] = upper
        shares_ref[k, 16:32, :] = last


def mid_pass(dev, flist, fcount, tlist, own, other, packed):
    return pl.pallas_call(
        mid_kernel,
        out_shape=[
            jax.ShapeDtypeStruct((32, 64), F32),
            jax.ShapeDtypeStruct((8, 32, 128), F32),
        ],
        in_specs=smem(4) + vmem(2) + hbm(1),
        out_specs=vmem(2),
        scratch_shapes=[
            pltpu.VMEM((120, 32, 128), BF16),
            pltpu.VMEM((PACKED, 128), BF16),
            pltpu.SemaphoreType.DMA,
        ],
        compiler_params=pltpu.CompilerParams(vmem_limit_bytes=GRANT - 16 * 1024 * 1024),
        cost_estimate=pl.CostEstimate(flops=300_000_000, bytes_accessed=5_000_000, transcendentals=0),
        name="mid_pass",
    )(dev, flist, fcount, tlist, own, other, packed)


def down_kernel(
    id_ref, mid_hbm, shares_hbm, path_hbm, dt_hbm, lt_hbm, basis_hbm, near_a_hbm, near_b_hbm,
    out_ref, mid_ref, shares_ref, path_ref, dt_ref, lt_ref, basis_ref, near_a, near_b, sems,
):
    moves = copies(
        (mid_hbm, shares_hbm, path_hbm, dt_hbm, lt_hbm, basis_hbm, near_a_hbm, near_b_hbm),
        (mid_ref, shares_ref, path_ref, dt_ref, lt_ref, basis_ref, near_a, near_b),
        sems,
    )
    for move in moves:
        move.start()
    for move in moves[:4]:
        move.wait()
    zl = (id_ref[0] >> 3) & 3
    upper = jnp.zeros((16, 128), F32)
    down = jnp.zeros((16, 64), F32)
    low = lax.broadcasted_iota(jnp.int32, (16, 128), 1) < 64
    for o in range(8):
        pair = jnp.where((o >> 1) == zl, 1.0, 0.0)
        quad = jnp.where((o >> 2) == (zl >> 1), 1.0, 0.0)
        upper = upper + shares_ref[o, 0:16, :] * jnp.where(low, pair, quad)
        down = down + shares_ref[o, 16:32, 0:64]
    down = upper[:, 64:128] + wide_dot(down, path_ref[2], NN)
    down = upper[:, 0:64] + wide_dot(down, path_ref[1], NN)
    down = mid_ref[0:16, :] + wide_dot(down, path_ref[0], NN)
    down = mid_ref[16:32, :] + wide_dot(down, dt_ref[0], NN)
    for move in moves[4:]:
        move.wait()
    near_refs = (near_a, near_b)
    near_blocks = [(ref, k) for ref in near_refs for k in range(ref.shape[1] // 256)]
    for leaf in range(16):
        near_ref, k = near_blocks[leaf]
        leaf_down = wide_dot(down, lt_ref[leaf], NN).astype(BF16)
        cols = slice(leaf * 256, (leaf + 1) * 256)
        near = near_ref[:, k * 256 : (k + 1) * 256]
        out_ref[:, cols] = near + dot(leaf_down, basis_ref[leaf], NN)


def down_pass(dev, mid, shares, path, dt, lt, basis, near):
    return pl.pallas_call(
        down_kernel,
        out_shape=jax.ShapeDtypeStruct((16, 4096), F32),
        in_specs=smem(1) + hbm(8),
        out_specs=vmem(1)[0],
        scratch_shapes=[
            pltpu.VMEM((32, 64), F32),
            pltpu.VMEM((8, 32, 128), F32),
            pltpu.VMEM((3, 64, 64), BF16),
            pltpu.VMEM((1, 64, 64), BF16),
            pltpu.VMEM((16, 64, 64), BF16),
            pltpu.VMEM((16, 64, 256), BF16),
            pltpu.VMEM(near[0].shape, F32),
            pltpu.VMEM(near[1].shape, F32),
            pltpu.SemaphoreType.DMA((8,)),
        ],
        compiler_params=pltpu.CompilerParams(vmem_limit_bytes=GRANT),
        cost_estimate=pl.CostEstimate(flops=20_000_000, bytes_accessed=1_500_000, transcendentals=0),
        name="down_pass",
    )(dev, mid, shares, path, dt, lt, basis, *near)


def cyclic(value, axis, size, by):
    return lax.ppermute(value, axis, [(i, (i + by) % size) for i in range(size)])


def spread(value, axis, size):
    rows = value.shape[0]
    same = jnp.broadcast_to(value[None], (size, rows, 128))
    return lax.all_to_all(same, axis, 0, 0, tiled=True).reshape(size * rows, 128)


def on_device(
    rhs, coords, basis, lt, dt, t1, t2, t3, far_list, far_count, far_coupling, top_list, top_coupling,
    near_list,
):
    dev = lax.axis_index(DEV).astype(jnp.int32).reshape(1)
    tie = lax.optimization_barrier
    payload, own = up_pass(dev, rhs, coords, basis, lt, dt)
    blocks = lax.all_to_all(payload, ("zh", "zl"), 0, 0, tiled=True).reshape(256, 128)
    swap_a = lax.ppermute(own, DEV, [(i, i ^ 1) for i in range(512)])
    swap_b = lax.ppermute(own, DEV, [(i, ((i + 1) ^ 1) - 1) for i in range(1, 511)] + [(0, 511), (511, 0)])
    own, t1 = tie((own, t1))
    packed, path = prep_pass(dev, t1, t2, t3, far_coupling, top_coupling)
    blocks, swap_a, swap_b, packed = tie((blocks, swap_a, swap_b, packed))
    near_list = jnp.transpose(near_list)
    gathered = spread(blocks, ("x", "y"), 16)
    near_a = near_field(dev, near_list, swap_a, own, swap_b, 0, 8)
    gathered, near_a, packed = tie((gathered, near_a, packed))
    other = cyclic(gathered, "core", 2, 1)
    mid, shares = mid_pass(dev, far_list, far_count, top_list, gathered, other, packed)
    shares, dev_b = tie((shares, dev))
    near_b = near_field(dev_b, near_list, swap_a, own, swap_b, 8, 16)
    shares = lax.all_to_all(shares, ("zl", "core"), 0, 0, tiled=True)
    return down_pass(dev, mid, shares, path, dt, lt, basis, (near_a, near_b))


def solution(mesh):
    torus = Mesh(mesh.devices.reshape(4, 4, 4, 2, 4), DEV)
    branch = DEV[:4]
    in_specs = (
        P(None, DEV),
        P(None, DEV),
        P(DEV, None, None),
        P(DEV, None, None),
        P(DEV, None, None),
        P(),
        P(),
        P(),
        P(DEV, None),
        P(DEV),
        P(DEV, None, None, None),
        P(branch, None, None),
        P(branch, None, None, None, None),
        P(DEV, None),
    )
    return jax.shard_map(
        on_device, mesh=torus, in_specs=in_specs, out_specs=P(None, DEV), check_vma=False
    )
```

```python
import functools

import jax
import jax.numpy as jnp
import numpy as np
from jax import lax
from jax.experimental import pallas as pl
from jax.experimental.pallas import tpu as pltpu
from jax.sharding import Mesh, PartitionSpec as P

F32 = jnp.float32
BF16 = jnp.bfloat16
DEV = ("x", "zh", "zl", "core", "y")
SCALE = float(20.0 * np.log2(np.e))
NT = (((1,), (1,)), ((), ()))
NN = (((1,), (0,)), ((), ()))
GRANT = 60 * 1024 * 1024
PACKED = 10240
ROOM = 98304


def dot(a, b, dims):
    return lax.dot_general(a, b, dims, preferred_element_type=F32)


def split(v):
    hi = v.astype(BF16)
    lo = (v - hi.astype(F32)).astype(BF16)
    return hi, lo


def wide_dot(v, b, dims):
    rows = v.shape[0]
    hi, lo = split(v)
    out = dot(jnp.concatenate([hi, lo], axis=0), b, dims)
    return out[:rows] + out[rows:]


def vmem(n):
    return [pl.BlockSpec(memory_space=pltpu.VMEM)] * n


def hbm(n):
    return [pl.BlockSpec(memory_space=pltpu.HBM)] * n


def smem(n):
    return [pl.BlockSpec(memory_space=pltpu.SMEM)] * n


def copies(sources, targets, sems):
    return [
        pltpu.make_async_copy(source, target, sems.at[k])
        for k, (source, target) in enumerate(zip(sources, targets))
    ]


def up_kernel(
    id_ref, rhs_hbm, coords_hbm, basis_hbm, lt_hbm, dt_hbm,
    out_ref, own_ref, rhs_ref, coords_ref, basis_ref, lt_ref, dt_ref, sems,
):
    moves = copies(
        (rhs_hbm, coords_hbm, basis_hbm, lt_hbm, dt_hbm),
        (rhs_ref, coords_ref, basis_ref, lt_ref, dt_ref),
        sems,
    )
    for move in moves:
        move.start()
    for move in moves:
        move.wait()
    total = jnp.zeros((16, 64), F32)
    for leaf in range(16):
        coeffs = dot(rhs_ref[:, leaf * 256 : (leaf + 1) * 256], basis_ref[leaf], NT)
        total = total + wide_dot(coeffs, lt_ref[leaf], NT)
    lifted = wide_dot(total, dt_ref[0], NT)
    even = (id_ref[0] >> 2) & 1 == 0
    first = jnp.where(even, lifted, total)
    second = jnp.where(even, total, lifted)
    both = jnp.concatenate([first, second], axis=1).astype(BF16)
    for k in range(16):
        out_ref[k] = both
    own_ref[0:16, :] = rhs_ref[...]
    xyz = coords_ref[...].astype(F32)
    own_ref[16:24, :] = jnp.concatenate([xyz, jnp.zeros((5, 4096), F32)], axis=0).astype(BF16)


def up_pass(dev, rhs, coords, basis, lt, dt):
    return pl.pallas_call(
        up_kernel,
        out_shape=[
            jax.ShapeDtypeStruct((16, 16, 128), BF16),
            jax.ShapeDtypeStruct((24, 4096), BF16),
        ],
        in_specs=smem(1) + hbm(5),
        out_specs=vmem(2),
        scratch_shapes=[
            pltpu.VMEM((16, 4096), BF16),
            pltpu.VMEM((3, 4096), BF16),
            pltpu.VMEM((16, 64, 256), BF16),
            pltpu.VMEM((16, 64, 64), BF16),
            pltpu.VMEM((1, 64, 64), BF16),
            pltpu.SemaphoreType.DMA((5,)),
        ],
        compiler_params=pltpu.CompilerParams(vmem_limit_bytes=GRANT),
        cost_estimate=pl.CostEstimate(flops=20_000_000, bytes_accessed=1_000_000, transcendentals=0),
        name="up_pass",
    )(dev, rhs, coords, basis, lt, dt)


def prepare(
    id_ref, t1_ref, t2_ref, t3_ref, fc_ref, tc_ref, packed_ref, path_ref
):
    def put(at, first, second):
        packed_ref[at * 64 : (at + 1) * 64, :] = jnp.concatenate([first, second], axis=1)

    for source, offset, nodes in ((t1_ref, 0, 64), (t2_ref, 64, 32), (t3_ref, 96, 16)):
        for n in range(nodes):
            put(offset + n, source[2 * n], source[2 * n + 1])
    for slot in range(16):
        put(112 + slot, fc_ref[0, slot], fc_ref[0, slot])
    for level in range(4):
        for slot in range(8):
            put(128 + level * 8 + slot, tc_ref[0, level, slot], tc_ref[0, level, slot])
    branch = id_ref[0] >> 2
    path_ref[0] = t2_ref[branch >> 1]
    path_ref[1] = t3_ref[branch >> 2]


def pick_kernel(id_ref, t1_hbm, out_hbm, sem):
    move = pltpu.make_async_copy(t1_hbm.at[pl.ds(id_ref[0] >> 2, 1)], out_hbm, sem)
    move.start()
    move.wait()


def pick_pass(dev, t1):
    return pl.pallas_call(
        pick_kernel,
        out_shape=jax.ShapeDtypeStruct((1, 64, 64), BF16),
        in_specs=smem(1) + hbm(1),
        out_specs=hbm(1)[0],
        scratch_shapes=[pltpu.SemaphoreType.DMA],
        compiler_params=pltpu.CompilerParams(vmem_limit_bytes=GRANT),
        cost_estimate=pl.CostEstimate(flops=0, bytes_accessed=32_000, transcendentals=0),
        name="pick_pass",
    )(dev, t1)


def features(xyz, centre):
    moved = (xyz - centre) * SCALE
    hi, lo = split(moved)
    exact = hi.astype(F32) + lo.astype(F32)
    norm = jnp.sum(exact * exact, axis=0, keepdims=True)
    n1 = norm.astype(BF16).astype(F32)
    n2 = (norm - n1).astype(BF16).astype(F32)
    n3 = norm - n1 - n2
    row = lax.broadcasted_iota(jnp.int32, xyz.shape, 0)
    norms = jnp.where(row == 0, n1, jnp.where(row == 1, n2, jnp.where(row == 2, n3, 0.0)))
    ones = jnp.where(row < 3, 1.0, 0.0)
    return hi.astype(F32), lo.astype(F32), norms, ones


def near_kernel(
    first, last, id_ref, near_ref, swap_a_ref, own_ref, swap_b_ref, out_ref, feat, rhs, target, between=None
):
    own_xyz = own_ref[16:24, :].astype(F32)
    low = jnp.min(own_xyz, axis=1, keepdims=True)
    high = jnp.max(own_xyz, axis=1, keepdims=True)
    centre = 0.5 * (low + high)
    for part, ref in enumerate((swap_a_ref, own_ref, swap_b_ref)):
        cols = pl.ds(part * 4096, 4096)
        rhs[:, cols] = ref[0:16, :]
        xyz = ref[16:24, :].astype(F32)
        hi, lo, norms, ones = features(xyz, centre)
        both = jnp.concatenate([hi, lo], axis=0).astype(BF16)
        feat[0:16, cols] = both
        feat[16:32, cols] = both
        feat[32:48, cols] = jnp.concatenate([ones, norms], axis=0).astype(BF16)
        if part == 1:
            for leaf in range(first, last):
                c = slice(leaf * 256, (leaf + 1) * 256)
                h = -2.0 * hi[:, c]
                m = -2.0 * lo[:, c]
                stack = jnp.concatenate([h, h, m, m, norms[:, c], ones[:, c]], axis=0)
                target[leaf - first] = jnp.transpose(stack).astype(BF16)
    if between is not None:
        between()
    base = (id_ref[0] - 1) * 16
    even = (id_ref[0] & 1) == 0

    def leaf_step(step, carry):
        left = target[step]
        total = jnp.zeros((16, 256), F32)
        for slot in range(8):
            source = near_ref[slot, first + step] - base
            source = jnp.minimum(jnp.maximum(source, 0), 47)
            part = source >> 4
            source = jnp.where(even, 2 - part, part) * 16 + (source & 15)
            cols = pl.ds(pl.multiple_of(source * 256, 256), 256)
            squared = jnp.maximum(dot(left, feat[:, cols], NN), 1e-20)
            tile = jnp.exp2(-(squared * lax.rsqrt(squared))).astype(BF16)
            total = total + dot(rhs[:, cols], tile, NT)
        out_ref[:, pl.ds(pl.multiple_of(step * 256, 256), 256)] = total
        return carry

    lax.fori_loop(0, last - first, leaf_step, 0, unroll=4)


def near_and_prep_kernel(
    first, last, id_ref, near_ref, swap_a_ref, own_ref, swap_b_ref, t1_hbm, t2_hbm, t3_hbm, fc_hbm, tc_hbm,
    out_ref, packed_hbm, path_ref,
    feat, rhs, target, packed, t1_ref, t2_ref, t3_ref, fc_ref, tc_ref, sems,
):
    moves = copies((t1_hbm, t2_hbm, t3_hbm, fc_hbm, tc_hbm), (t1_ref, t2_ref, t3_ref, fc_ref, tc_ref), sems)
    out = pltpu.make_async_copy(packed, packed_hbm.at[0:PACKED, :], sems.at[5])
    for move in moves:
        move.start()

    def between():
        for move in moves:
            move.wait()
        prepare(id_ref, t1_ref, t2_ref, t3_ref, fc_ref, tc_ref, packed, path_ref)
        out.start()

    near_kernel(
        first, last, id_ref, near_ref, swap_a_ref, own_ref, swap_b_ref, out_ref, feat, rhs, target, between
    )
    out.wait()


def near_cost(leaves):
    return pl.CostEstimate(
        flops=400_000_000 * leaves, bytes_accessed=600_000, transcendentals=1_050_000 * leaves
    )


def near_scratch(leaves):
    return [
        pltpu.VMEM((48, 12288), BF16),
        pltpu.VMEM((16, 12288), BF16),
        pltpu.VMEM((leaves, 256, 48), BF16),
    ]


def near_and_prep(dev, near_list, swap_a, own, swap_b, t1, t2, t3, fc, tc, first, last):
    return pl.pallas_call(
        functools.partial(near_and_prep_kernel, first, last),
        out_shape=[
            jax.ShapeDtypeStruct((16, (last - first) * 256), F32),
            jax.ShapeDtypeStruct((ROOM, 128), BF16),
            jax.ShapeDtypeStruct((2, 64, 64), BF16),
        ],
        in_specs=smem(2) + vmem(3) + hbm(5),
        out_specs=vmem(1) + hbm(1) + vmem(1),
        scratch_shapes=near_scratch(last - first)
        + [
            pltpu.VMEM((PACKED, 128), BF16),
            pltpu.VMEM((128, 64, 64), BF16),
            pltpu.VMEM((64, 64, 64), BF16),
            pltpu.VMEM((32, 64, 64), BF16),
            pltpu.VMEM((1, 16, 64, 64), BF16),
            pltpu.VMEM((1, 4, 8, 64, 64), BF16),
            pltpu.SemaphoreType.DMA((6,)),
        ],
        compiler_params=pltpu.CompilerParams(vmem_limit_bytes=GRANT),
        cost_estimate=near_cost(last - first + 2),
        name="near_and_prep",
    )(dev, near_list, swap_a, own, swap_b, t1, t2, t3, fc, tc)


def near_field(dev, near_list, swap_a, own, swap_b, first, last):
    return pl.pallas_call(
        functools.partial(near_kernel, first, last),
        out_shape=jax.ShapeDtypeStruct((16, (last - first) * 256), F32),
        in_specs=smem(2) + vmem(3),
        out_specs=vmem(1)[0],
        scratch_shapes=near_scratch(last - first),
        compiler_params=pltpu.CompilerParams(vmem_limit_bytes=GRANT),
        cost_estimate=near_cost(last - first + 1),
        name="near_field",
    )(dev, near_list, swap_a, own, swap_b)


def half_kernel(own_ref, packed_hbm, sums_ref, packed_ref, sem):
    move = pltpu.make_async_copy(packed_hbm.at[0:PACKED, :], packed_ref, sem)
    move.start()
    for x in range(4):
        parts = [own_ref[(x * 4 + y) * 256 : (x * 4 + y + 1) * 256, :].astype(F32) for y in range(4)]
        sums_ref[x * 256 : (x + 1) * 256, :] = (parts[0] + parts[1]) + (parts[2] + parts[3])
    move.wait()


def half_pass(own, packed):
    return pl.pallas_call(
        half_kernel,
        out_shape=[
            jax.ShapeDtypeStruct((1024, 128), F32),
            jax.ShapeDtypeStruct((PACKED, 128), BF16),
        ],
        in_specs=vmem(1) + hbm(1),
        out_specs=vmem(2),
        scratch_shapes=[pltpu.SemaphoreType.DMA],
        compiler_params=pltpu.CompilerParams(vmem_limit_bytes=GRANT - 16 * 1024 * 1024),
        cost_estimate=pl.CostEstimate(flops=1_000_000, bytes_accessed=5_000_000, transcendentals=0),
        name="half_pass",
    )(own, packed)


def mid_kernel(
    id_ref, flist_ref, fcount_ref, tlist_ref, own_ref, other_ref, sums_ref, packed,
    out_ref, shares_ref, nodes,
):
    my_core = (id_ref[0] >> 2) & 1
    lane16 = lax.broadcasted_iota(jnp.int32, (16, 128), 1)
    low16 = lane16 < 64
    half16 = jnp.where(low16, 0, 1)
    from_own = half16 == my_core

    def put(at, value):
        hi, lo = split(value)
        nodes[at] = jnp.concatenate([hi, lo], axis=0)

    def raise_four(pairs, weights):
        value = jnp.concatenate(pairs, axis=0)
        hi, lo = split(value)
        out = dot(jnp.concatenate([hi, lo], axis=0), weights, NT)
        out = out[:64] + out[64:]
        first = jnp.where(low16, out[0:16, 0:128], out[16:32, 0:128])
        second = jnp.where(low16, out[32:48, 128:256], out[48:64, 128:256])
        return first, second

    def side_by_side(first, count):
        return jnp.concatenate([packed[(first + k) * 64 : (first + k + 1) * 64, :] for k in range(count)], axis=1)

    ones = []
    for at_x in range(4):
        for z in range(16):
            at = (at_x * 64 + z) * 16
            parts = [other_ref[y * 256 + at : y * 256 + at + 16, :].astype(F32) for y in range(4)]
            other = (parts[0] + parts[1]) + (parts[2] + parts[3])
            row = (at_x * 16 + z) * 16
            ones.append(jnp.where(from_own, sums_ref[row : row + 16, :], other))
            put(at_x * 16 + z, ones[-1])
    for at_x in range(4):
        twos = []
        for quad in range(4):
            node = at_x * 16 + quad * 4
            twos.extend(raise_four(ones[node : node + 4], packed[node * 64 : node * 64 + 256, :]))
        for k in range(8):
            put(64 + at_x * 8 + k, twos[k])
        threes = []
        for quad in range(2):
            row = (64 + at_x * 8 + quad * 4) * 64
            threes.extend(raise_four(twos[quad * 4 : quad * 4 + 4], packed[row : row + 256, :]))
        for k in range(4):
            put(96 + at_x * 4 + k, threes[k])
        row = (96 + at_x * 4) * 64
        fours = raise_four(threes, packed[row : row + 256, :])
        for k in range(2):
            put(112 + at_x * 2 + k, fours[k])

    blocks = []
    for slot in range(16):
        c = flist_ref[0, slot]
        c_y, c_core = c & 3, (c >> 2) & 1
        place = pl.multiple_of((((c >> 7) * 4 + c_y) * 16 + ((c >> 3) & 15)) * 16, 16)
        block = jnp.where(c_core == my_core, own_ref[pl.ds(place, 16), :], other_ref[pl.ds(place, 16), :])
        live = jnp.where(slot < fcount_ref[0], 1 - c_core, 2)
        blocks.append(block * jnp.where(half16 == live, 1.0, 0.0).astype(BF16))
    out_ref[16:32, :] = dot(jnp.concatenate(blocks, axis=1), side_by_side(112, 16), NT)

    parts = []
    for level, offset in enumerate((0, 64, 96, 112)):
        blocks = []
        for slot in range(8):
            node = tlist_ref[0, level, slot]
            block = nodes[offset + (node >> 1)]
            mask = jnp.where(half16 == (node & 1), 1.0, 0.0).astype(BF16)
            blocks.append(block * jnp.concatenate([mask, mask], axis=0))
        out = dot(jnp.concatenate(blocks, axis=1), side_by_side(128 + level * 8, 8), NT)
        parts.append(out[:16] + out[16:])
    out_ref[0:16, :] = parts[0]
    upper = jnp.concatenate([parts[1], parts[2]], axis=1)
    last = jnp.concatenate([parts[3], parts[3]], axis=1)
    for k in range(8):
        shares_ref[k, 0:16, :] = upper
        shares_ref[k, 16:32, :] = last


def mid_pass(dev, flist, fcount, tlist, own, other, sums, packed):
    return pl.pallas_call(
        mid_kernel,
        out_shape=[
            jax.ShapeDtypeStruct((32, 64), F32),
            jax.ShapeDtypeStruct((8, 32, 128), F32),
        ],
        in_specs=smem(4) + vmem(4),
        out_specs=vmem(2),
        scratch_shapes=[pltpu.VMEM((120, 32, 128), BF16)],
        compiler_params=pltpu.CompilerParams(vmem_limit_bytes=GRANT - 16 * 1024 * 1024),
        cost_estimate=pl.CostEstimate(flops=300_000_000, bytes_accessed=5_000_000, transcendentals=0),
        name="mid_pass",
    )(dev, flist, fcount, tlist, own, other, sums, packed)


def down_kernel(
    id_ref, mid_hbm, shares_hbm, path_hbm, one_hbm, dt_hbm, lt_hbm, basis_hbm, near_a_hbm, near_b_hbm,
    out_ref, mid_ref, shares_ref, path_ref, one_ref, dt_ref, lt_ref, basis_ref, near_a, near_b, sems,
):
    moves = copies(
        (mid_hbm, shares_hbm, path_hbm, one_hbm, dt_hbm, lt_hbm, basis_hbm, near_a_hbm, near_b_hbm),
        (mid_ref, shares_ref, path_ref, one_ref, dt_ref, lt_ref, basis_ref, near_a, near_b),
        sems,
    )
    for move in moves:
        move.start()
    for move in moves[:5]:
        move.wait()
    zl = (id_ref[0] >> 3) & 3
    upper = jnp.zeros((16, 128), F32)
    down = jnp.zeros((16, 64), F32)
    low = lax.broadcasted_iota(jnp.int32, (16, 128), 1) < 64
    for o in range(8):
        pair = jnp.where((o >> 1) == zl, 1.0, 0.0)
        quad = jnp.where((o >> 2) == (zl >> 1), 1.0, 0.0)
        upper = upper + shares_ref[o, 0:16, :] * jnp.where(low, pair, quad)
        down = down + shares_ref[o, 16:32, 0:64]
    down = upper[:, 64:128] + wide_dot(down, path_ref[1], NN)
    down = upper[:, 0:64] + wide_dot(down, path_ref[0], NN)
    down = mid_ref[0:16, :] + wide_dot(down, one_ref[0], NN)
    down = mid_ref[16:32, :] + wide_dot(down, dt_ref[0], NN)
    for move in moves[5:]:
        move.wait()
    near_refs = (near_a, near_b)
    near_blocks = [(ref, k) for ref in near_refs for k in range(ref.shape[1] // 256)]
    for leaf in range(16):
        near_ref, k = near_blocks[leaf]
        leaf_down = wide_dot(down, lt_ref[leaf], NN).astype(BF16)
        cols = slice(leaf * 256, (leaf + 1) * 256)
        near = near_ref[:, k * 256 : (k + 1) * 256]
        out_ref[:, cols] = near + dot(leaf_down, basis_ref[leaf], NN)


def down_pass(dev, mid, shares, path, one, dt, lt, basis, near):
    return pl.pallas_call(
        down_kernel,
        out_shape=jax.ShapeDtypeStruct((16, 4096), F32),
        in_specs=smem(1) + hbm(9),
        out_specs=vmem(1)[0],
        scratch_shapes=[
            pltpu.VMEM((32, 64), F32),
            pltpu.VMEM((8, 32, 128), F32),
            pltpu.VMEM((2, 64, 64), BF16),
            pltpu.VMEM((1, 64, 64), BF16),
            pltpu.VMEM((1, 64, 64), BF16),
            pltpu.VMEM((16, 64, 64), BF16),
            pltpu.VMEM((16, 64, 256), BF16),
            pltpu.VMEM(near[0].shape, F32),
            pltpu.VMEM(near[1].shape, F32),
            pltpu.SemaphoreType.DMA((9,)),
        ],
        compiler_params=pltpu.CompilerParams(vmem_limit_bytes=GRANT),
        cost_estimate=pl.CostEstimate(flops=20_000_000, bytes_accessed=1_500_000, transcendentals=0),
        name="down_pass",
    )(dev, mid, shares, path, one, dt, lt, basis, *near)


def cyclic(value, axis, size, by):
    return lax.ppermute(value, axis, [(i, (i + by) % size) for i in range(size)])


def spread(value, axis, size):
    rows = value.shape[0]
    same = jnp.broadcast_to(value[None], (size, rows, 128))
    return lax.all_to_all(same, axis, 0, 0, tiled=True).reshape(size * rows, 128)


def on_device(
    rhs, coords, basis, lt, dt, t1, t2, t3, far_list, far_count, far_coupling, top_list, top_coupling,
    near_list,
):
    dev = lax.axis_index(DEV).astype(jnp.int32).reshape(1)
    tie = lax.optimization_barrier
    payload, own = up_pass(dev, rhs, coords, basis, lt, dt)
    blocks = lax.all_to_all(payload, ("zh", "zl"), 0, 0, tiled=True).reshape(256, 128)
    swap_a = lax.ppermute(own, DEV, [(i, i ^ 1) for i in range(512)])
    swap_b = lax.ppermute(own, DEV, [(i, ((i + 1) ^ 1) - 1) for i in range(1, 511)] + [(0, 511), (511, 0)])
    own, t1 = tie((own, t1))
    one = pick_pass(dev, t1)
    blocks, swap_a, swap_b, one = tie((blocks, swap_a, swap_b, one))
    near_list = jnp.transpose(near_list)
    gathered = spread(blocks, ("x", "y"), 16)
    near_a, packed, path = near_and_prep(
        dev, near_list, swap_a, own, swap_b, t1, t2, t3, far_coupling, top_coupling, 0, 12
    )
    gathered, near_a, packed = tie((gathered, near_a, packed))
    other = cyclic(gathered, "core", 2, 1)
    sums, packed = half_pass(gathered, packed)
    mid, shares = mid_pass(dev, far_list, far_count, top_list, gathered, other, sums, packed)
    shares, dev_b = tie((shares, dev))
    near_b = near_field(dev_b, near_list, swap_a, own, swap_b, 12, 16)
    shares = lax.all_to_all(shares, ("zl", "core"), 0, 0, tiled=True)
    return down_pass(dev, mid, shares, path, one, dt, lt, basis, (near_a, near_b))


def solution(mesh):
    torus = Mesh(mesh.devices.reshape(4, 4, 4, 2, 4), DEV)
    branch = DEV[:4]
    in_specs = (
        P(None, DEV),
        P(None, DEV),
        P(DEV, None, None),
        P(DEV, None, None),
        P(DEV, None, None),
        P(),
        P(),
        P(),
        P(DEV, None),
        P(DEV),
        P(DEV, None, None, None),
        P(branch, None, None),
        P(branch, None, None, None, None),
        P(DEV, None),
    )
    return jax.shard_map(
        on_device, mesh=torus, in_specs=in_specs, out_specs=P(None, DEV), check_vma=False
    )
```

```python
import functools

import jax
import jax.numpy as jnp
import numpy as np
from jax import lax
from jax.experimental import pallas as pl
from jax.experimental.pallas import tpu as pltpu
from jax.sharding import Mesh, PartitionSpec as P

F32 = jnp.float32
BF16 = jnp.bfloat16
DEV = ("x", "zh", "zl", "core", "y")
SCALE = float(20.0 * np.log2(np.e))
NT = (((1,), (1,)), ((), ()))
NN = (((1,), (0,)), ((), ()))
GRANT = 60 * 1024 * 1024
PACKED = 10240
ROOM = 98304


def dot(a, b, dims):
    return lax.dot_general(a, b, dims, preferred_element_type=F32)


def split(v):
    hi = v.astype(BF16)
    lo = (v - hi.astype(F32)).astype(BF16)
    return hi, lo


def wide_dot(v, b, dims):
    rows = v.shape[0]
    hi, lo = split(v)
    out = dot(jnp.concatenate([hi, lo], axis=0), b, dims)
    return out[:rows] + out[rows:]


def vmem(n):
    return [pl.BlockSpec(memory_space=pltpu.VMEM)] * n


def hbm(n):
    return [pl.BlockSpec(memory_space=pltpu.HBM)] * n


def smem(n):
    return [pl.BlockSpec(memory_space=pltpu.SMEM)] * n


def copies(sources, targets, sems):
    return [
        pltpu.make_async_copy(source, target, sems.at[k])
        for k, (source, target) in enumerate(zip(sources, targets))
    ]


def up_kernel(
    id_ref, rhs_hbm, coords_hbm, basis_hbm, lt_hbm, dt_hbm,
    out_ref, own_ref, rhs_ref, coords_ref, basis_ref, lt_ref, dt_ref, sems,
):
    moves = copies(
        (rhs_hbm, coords_hbm, basis_hbm, lt_hbm, dt_hbm),
        (rhs_ref, coords_ref, basis_ref, lt_ref, dt_ref),
        sems,
    )
    for move in moves:
        move.start()
    for move in moves:
        move.wait()
    total = jnp.zeros((16, 64), F32)
    for leaf in range(16):
        coeffs = dot(rhs_ref[:, leaf * 256 : (leaf + 1) * 256], basis_ref[leaf], NT)
        total = total + wide_dot(coeffs, lt_ref[leaf], NT)
    lifted = wide_dot(total, dt_ref[0], NT)
    even = (id_ref[0] >> 2) & 1 == 0
    first = jnp.where(even, lifted, total)
    second = jnp.where(even, total, lifted)
    both = jnp.concatenate([first, second], axis=1).astype(BF16)
    for k in range(16):
        out_ref[k] = both
    own_ref[0:16, :] = rhs_ref[...]
    xyz = coords_ref[...].astype(F32)
    own_ref[16:24, :] = jnp.concatenate([xyz, jnp.zeros((5, 4096), F32)], axis=0).astype(BF16)


def up_pass(dev, rhs, coords, basis, lt, dt):
    return pl.pallas_call(
        up_kernel,
        out_shape=[
            jax.ShapeDtypeStruct((16, 16, 128), BF16),
            jax.ShapeDtypeStruct((24, 4096), BF16),
        ],
        in_specs=smem(1) + hbm(5),
        out_specs=vmem(2),
        scratch_shapes=[
            pltpu.VMEM((16, 4096), BF16),
            pltpu.VMEM((3, 4096), BF16),
            pltpu.VMEM((16, 64, 256), BF16),
            pltpu.VMEM((16, 64, 64), BF16),
            pltpu.VMEM((1, 64, 64), BF16),
            pltpu.SemaphoreType.DMA((5,)),
        ],
        compiler_params=pltpu.CompilerParams(vmem_limit_bytes=GRANT),
        cost_estimate=pl.CostEstimate(flops=20_000_000, bytes_accessed=1_000_000, transcendentals=0),
        name="up_pass",
    )(dev, rhs, coords, basis, lt, dt)


def prepare(
    id_ref, t1_ref, t2_ref, t3_ref, fc_ref, tc_ref, packed_ref, path_ref
):
    def put(at, first, second):
        packed_ref[at * 64 : (at + 1) * 64, :] = jnp.concatenate([first, second], axis=1)

    for source, offset, nodes in ((t1_ref, 0, 64), (t2_ref, 64, 32), (t3_ref, 96, 16)):
        for n in range(nodes):
            put(offset + n, source[2 * n], source[2 * n + 1])
    for slot in range(16):
        put(112 + slot, fc_ref[0, slot], fc_ref[0, slot])
    for level in range(4):
        for slot in range(8):
            put(128 + level * 8 + slot, tc_ref[0, level, slot], tc_ref[0, level, slot])
    branch = id_ref[0] >> 2
    path_ref[0] = t1_ref[branch]
    path_ref[1] = t2_ref[branch >> 1]
    path_ref[2] = t3_ref[branch >> 2]


def order_kernel(id_ref, t1_hbm, out_ref):
    out_ref[0] = id_ref[0]


def order_pass(dev, t1):
    return pl.pallas_call(
        order_kernel,
        out_shape=jax.ShapeDtypeStruct((1,), jnp.int32),
        in_specs=smem(1) + hbm(1),
        out_specs=smem(1)[0],
        compiler_params=pltpu.CompilerParams(vmem_limit_bytes=GRANT),
        cost_estimate=pl.CostEstimate(flops=0, bytes_accessed=64, transcendentals=0),
        name="order_pass",
    )(dev, t1)


def features(xyz, centre):
    moved = (xyz - centre) * SCALE
    hi, lo = split(moved)
    exact = hi.astype(F32) + lo.astype(F32)
    norm = jnp.sum(exact * exact, axis=0, keepdims=True)
    n1 = norm.astype(BF16).astype(F32)
    n2 = (norm - n1).astype(BF16).astype(F32)
    n3 = norm - n1 - n2
    row = lax.broadcasted_iota(jnp.int32, xyz.shape, 0)
    norms = jnp.where(row == 0, n1, jnp.where(row == 1, n2, jnp.where(row == 2, n3, 0.0)))
    ones = jnp.where(row < 3, 1.0, 0.0)
    return hi.astype(F32), lo.astype(F32), norms, ones


def near_kernel(
    first, last, id_ref, near_ref, swap_a_ref, own_ref, swap_b_ref, out_ref, feat, rhs, target, between=None
):
    own_xyz = own_ref[16:24, :].astype(F32)
    low = jnp.min(own_xyz, axis=1, keepdims=True)
    high = jnp.max(own_xyz, axis=1, keepdims=True)
    centre = 0.5 * (low + high)
    for part, ref in enumerate((swap_a_ref, own_ref, swap_b_ref)):
        cols = pl.ds(part * 4096, 4096)
        rhs[:, cols] = ref[0:16, :]
        xyz = ref[16:24, :].astype(F32)
        hi, lo, norms, ones = features(xyz, centre)
        both = jnp.concatenate([hi, lo], axis=0).astype(BF16)
        feat[0:16, cols] = both
        feat[16:32, cols] = both
        feat[32:48, cols] = jnp.concatenate([ones, norms], axis=0).astype(BF16)
        if part == 1:
            for leaf in range(first, last):
                c = slice(leaf * 256, (leaf + 1) * 256)
                h = -2.0 * hi[:, c]
                m = -2.0 * lo[:, c]
                stack = jnp.concatenate([h, h, m, m, norms[:, c], ones[:, c]], axis=0)
                target[leaf - first] = jnp.transpose(stack).astype(BF16)
    if between is not None:
        between()
    base = (id_ref[0] - 1) * 16
    even = (id_ref[0] & 1) == 0

    def leaf_step(step, carry):
        left = target[step]
        total = jnp.zeros((16, 256), F32)
        for slot in range(8):
            source = near_ref[slot, first + step] - base
            source = jnp.minimum(jnp.maximum(source, 0), 47)
            part = source >> 4
            source = jnp.where(even, 2 - part, part) * 16 + (source & 15)
            cols = pl.ds(pl.multiple_of(source * 256, 256), 256)
            squared = jnp.maximum(dot(left, feat[:, cols], NN), 1e-20)
            tile = jnp.exp2(-(squared * lax.rsqrt(squared))).astype(BF16)
            total = total + dot(rhs[:, cols], tile, NT)
        out_ref[:, pl.ds(pl.multiple_of(step * 256, 256), 256)] = total
        return carry

    lax.fori_loop(0, last - first, leaf_step, 0, unroll=min(6, last - first))


def near_and_prep_kernel(
    first, last, id_ref, near_ref, swap_a_ref, own_ref, swap_b_ref, t1_hbm, t2_hbm, t3_hbm, fc_hbm, tc_hbm,
    out_ref, packed_hbm, path_ref,
    feat, rhs, target, packed, t1_ref, t2_ref, t3_ref, fc_ref, tc_ref, sems,
):
    moves = copies((t1_hbm, t2_hbm, t3_hbm, fc_hbm, tc_hbm), (t1_ref, t2_ref, t3_ref, fc_ref, tc_ref), sems)
    out = pltpu.make_async_copy(packed, packed_hbm.at[0:PACKED, :], sems.at[5])
    for move in moves:
        move.start()

    def between():
        for move in moves:
            move.wait()
        prepare(id_ref, t1_ref, t2_ref, t3_ref, fc_ref, tc_ref, packed, path_ref)
        out.start()

    near_kernel(
        first, last, id_ref, near_ref, swap_a_ref, own_ref, swap_b_ref, out_ref, feat, rhs, target, between
    )
    out.wait()


def near_cost(leaves):
    return pl.CostEstimate(
        flops=400_000_000 * leaves, bytes_accessed=600_000, transcendentals=1_050_000 * leaves
    )


def near_scratch(leaves):
    return [
        pltpu.VMEM((48, 12288), BF16),
        pltpu.VMEM((16, 12288), BF16),
        pltpu.VMEM((leaves, 256, 48), BF16),
    ]


def near_and_prep(dev, near_list, swap_a, own, swap_b, t1, t2, t3, fc, tc, first, last):
    return pl.pallas_call(
        functools.partial(near_and_prep_kernel, first, last),
        out_shape=[
            jax.ShapeDtypeStruct((16, (last - first) * 256), F32),
            jax.ShapeDtypeStruct((ROOM, 128), BF16),
            jax.ShapeDtypeStruct((3, 64, 64), BF16),
        ],
        in_specs=smem(2) + vmem(3) + hbm(5),
        out_specs=vmem(1) + hbm(1) + vmem(1),
        scratch_shapes=near_scratch(last - first)
        + [
            pltpu.VMEM((PACKED, 128), BF16),
            pltpu.VMEM((128, 64, 64), BF16),
            pltpu.VMEM((64, 64, 64), BF16),
            pltpu.VMEM((32, 64, 64), BF16),
            pltpu.VMEM((1, 16, 64, 64), BF16),
            pltpu.VMEM((1, 4, 8, 64, 64), BF16),
            pltpu.SemaphoreType.DMA((6,)),
        ],
        compiler_params=pltpu.CompilerParams(vmem_limit_bytes=GRANT),
        cost_estimate=near_cost(last - first + 2),
        name="near_and_prep",
    )(dev, near_list, swap_a, own, swap_b, t1, t2, t3, fc, tc)


def near_field(dev, near_list, swap_a, own, swap_b, first, last):
    return pl.pallas_call(
        functools.partial(near_kernel, first, last),
        out_shape=jax.ShapeDtypeStruct((16, (last - first) * 256), F32),
        in_specs=smem(2) + vmem(3),
        out_specs=vmem(1)[0],
        scratch_shapes=near_scratch(last - first),
        compiler_params=pltpu.CompilerParams(vmem_limit_bytes=GRANT),
        cost_estimate=near_cost(last - first + 1),
        name="near_field",
    )(dev, near_list, swap_a, own, swap_b)


def half_kernel(own_ref, packed_hbm, sums_ref, packed_ref, sem):
    move = pltpu.make_async_copy(packed_hbm.at[0:PACKED, :], packed_ref, sem)
    move.start()
    for x in range(4):
        parts = [own_ref[(x * 4 + y) * 256 : (x * 4 + y + 1) * 256, :].astype(F32) for y in range(4)]
        sums_ref[x * 256 : (x + 1) * 256, :] = (parts[0] + parts[1]) + (parts[2] + parts[3])
    move.wait()


def half_pass(own, packed):
    return pl.pallas_call(
        half_kernel,
        out_shape=[
            jax.ShapeDtypeStruct((1024, 128), F32),
            jax.ShapeDtypeStruct((PACKED, 128), BF16),
        ],
        in_specs=vmem(1) + hbm(1),
        out_specs=vmem(2),
        scratch_shapes=[pltpu.SemaphoreType.DMA],
        compiler_params=pltpu.CompilerParams(vmem_limit_bytes=GRANT - 16 * 1024 * 1024),
        cost_estimate=pl.CostEstimate(flops=1_000_000, bytes_accessed=5_000_000, transcendentals=0),
        name="half_pass",
    )(own, packed)


def mid_kernel(
    id_ref, flist_ref, fcount_ref, tlist_ref, own_ref, other_ref, sums_ref, packed,
    shares_ref, nodes,
):
    my_core = (id_ref[0] >> 2) & 1
    lane16 = lax.broadcasted_iota(jnp.int32, (16, 128), 1)
    low16 = lane16 < 64
    half16 = jnp.where(low16, 0, 1)
    from_own = half16 == my_core

    def put(at, value):
        hi, lo = split(value)
        nodes[at] = jnp.concatenate([hi, lo], axis=0)

    def raise_four(pairs, weights):
        value = jnp.concatenate(pairs, axis=0)
        hi, lo = split(value)
        out = dot(jnp.concatenate([hi, lo], axis=0), weights, NT)
        out = out[:64] + out[64:]
        first = jnp.where(low16, out[0:16, 0:128], out[16:32, 0:128])
        second = jnp.where(low16, out[32:48, 128:256], out[48:64, 128:256])
        return first, second

    def side_by_side(first, count):
        return jnp.concatenate([packed[(first + k) * 64 : (first + k + 1) * 64, :] for k in range(count)], axis=1)

    ones = []
    for at_x in range(4):
        for z in range(16):
            at = (at_x * 64 + z) * 16
            parts = [other_ref[y * 256 + at : y * 256 + at + 16, :].astype(F32) for y in range(4)]
            other = (parts[0] + parts[1]) + (parts[2] + parts[3])
            row = (at_x * 16 + z) * 16
            ones.append(jnp.where(from_own, sums_ref[row : row + 16, :], other))
            put(at_x * 16 + z, ones[-1])
    for at_x in range(4):
        twos = []
        for quad in range(4):
            node = at_x * 16 + quad * 4
            twos.extend(raise_four(ones[node : node + 4], packed[node * 64 : node * 64 + 256, :]))
        for k in range(8):
            put(64 + at_x * 8 + k, twos[k])
        threes = []
        for quad in range(2):
            row = (64 + at_x * 8 + quad * 4) * 64
            threes.extend(raise_four(twos[quad * 4 : quad * 4 + 4], packed[row : row + 256, :]))
        for k in range(4):
            put(96 + at_x * 4 + k, threes[k])
        row = (96 + at_x * 4) * 64
        fours = raise_four(threes, packed[row : row + 256, :])
        for k in range(2):
            put(112 + at_x * 2 + k, fours[k])

    blocks = []
    for slot in range(16):
        c = flist_ref[0, slot]
        c_y, c_core = c & 3, (c >> 2) & 1
        place = pl.multiple_of((((c >> 7) * 4 + c_y) * 16 + ((c >> 3) & 15)) * 16, 16)
        block = jnp.where(c_core == my_core, own_ref[pl.ds(place, 16), :], other_ref[pl.ds(place, 16), :])
        live = jnp.where(slot < fcount_ref[0], 1 - c_core, 2)
        blocks.append(block * jnp.where(half16 == live, 1.0, 0.0).astype(BF16))
    far = dot(jnp.concatenate(blocks, axis=1), side_by_side(112, 16), NT)

    parts = []
    for level, offset in enumerate((0, 64, 96, 112)):
        blocks = []
        for slot in range(8):
            node = tlist_ref[0, level, slot]
            block = nodes[offset + (node >> 1)]
            mask = jnp.where(half16 == (node & 1), 1.0, 0.0).astype(BF16)
            blocks.append(block * jnp.concatenate([mask, mask], axis=0))
        out = dot(jnp.concatenate(blocks, axis=1), side_by_side(128 + level * 8, 8), NT)
        parts.append(out[:16] + out[16:])
    upper = jnp.concatenate([parts[1], parts[2]], axis=1)
    last = jnp.concatenate([parts[3], parts[0]], axis=1)
    far = jnp.concatenate([far, far], axis=1)
    for k in range(8):
        shares_ref[k, 0:16, :] = upper
        shares_ref[k, 16:32, :] = last
        shares_ref[k, 32:48, :] = far


def mid_pass(dev, flist, fcount, tlist, own, other, sums, packed):
    return pl.pallas_call(
        mid_kernel,
        out_shape=jax.ShapeDtypeStruct((8, 48, 128), F32),
        in_specs=smem(4) + vmem(4),
        out_specs=vmem(1)[0],
        scratch_shapes=[pltpu.VMEM((120, 32, 128), BF16)],
        compiler_params=pltpu.CompilerParams(vmem_limit_bytes=GRANT - 16 * 1024 * 1024),
        cost_estimate=pl.CostEstimate(flops=300_000_000, bytes_accessed=5_000_000, transcendentals=0),
        name="mid_pass",
    )(dev, flist, fcount, tlist, own, other, sums, packed)


def down_kernel(
    id_ref, shares_hbm, path_hbm, dt_hbm, lt_hbm, basis_hbm, near_a_hbm, near_b_hbm,
    out_ref, shares_ref, path_ref, dt_ref, lt_ref, basis_ref, near_a, near_b, sems,
):
    moves = copies(
        (shares_hbm, path_hbm, dt_hbm, lt_hbm, basis_hbm, near_a_hbm, near_b_hbm),
        (shares_ref, path_ref, dt_ref, lt_ref, basis_ref, near_a, near_b),
        sems,
    )
    for move in moves:
        move.start()
    for move in moves[:3]:
        move.wait()
    zl = (id_ref[0] >> 3) & 3
    mine = shares_ref[(id_ref[0] >> 2) & 7]
    upper = jnp.zeros((16, 128), F32)
    down = jnp.zeros((16, 64), F32)
    low = lax.broadcasted_iota(jnp.int32, (16, 128), 1) < 64
    for o in range(8):
        pair = jnp.where((o >> 1) == zl, 1.0, 0.0)
        quad = jnp.where((o >> 2) == (zl >> 1), 1.0, 0.0)
        upper = upper + shares_ref[o, 0:16, :] * jnp.where(low, pair, quad)
        down = down + shares_ref[o, 16:32, 0:64]
    down = upper[:, 64:128] + wide_dot(down, path_ref[2], NN)
    down = upper[:, 0:64] + wide_dot(down, path_ref[1], NN)
    down = mine[16:32, 64:128] + wide_dot(down, path_ref[0], NN)
    down = mine[32:48, 0:64] + wide_dot(down, dt_ref[0], NN)
    for move in moves[3:]:
        move.wait()
    near_refs = (near_a, near_b)
    near_blocks = [(ref, k) for ref in near_refs for k in range(ref.shape[1] // 256)]
    for leaf in range(16):
        near_ref, k = near_blocks[leaf]
        leaf_down = wide_dot(down, lt_ref[leaf], NN).astype(BF16)
        cols = slice(leaf * 256, (leaf + 1) * 256)
        near = near_ref[:, k * 256 : (k + 1) * 256]
        out_ref[:, cols] = near + dot(leaf_down, basis_ref[leaf], NN)


def down_pass(dev, shares, path, dt, lt, basis, near):
    return pl.pallas_call(
        down_kernel,
        out_shape=jax.ShapeDtypeStruct((16, 4096), F32),
        in_specs=smem(1) + hbm(7),
        out_specs=vmem(1)[0],
        scratch_shapes=[
            pltpu.VMEM((8, 48, 128), F32),
            pltpu.VMEM((3, 64, 64), BF16),
            pltpu.VMEM((1, 64, 64), BF16),
            pltpu.VMEM((16, 64, 64), BF16),
            pltpu.VMEM((16, 64, 256), BF16),
            pltpu.VMEM(near[0].shape, F32),
            pltpu.VMEM(near[1].shape, F32),
            pltpu.SemaphoreType.DMA((7,)),
        ],
        compiler_params=pltpu.CompilerParams(vmem_limit_bytes=GRANT),
        cost_estimate=pl.CostEstimate(flops=20_000_000, bytes_accessed=1_500_000, transcendentals=0),
        name="down_pass",
    )(dev, shares, path, dt, lt, basis, *near)


def cyclic(value, axis, size, by):
    return lax.ppermute(value, axis, [(i, (i + by) % size) for i in range(size)])


def spread(value, axis, size):
    rows = value.shape[0]
    same = jnp.broadcast_to(value[None], (size, rows, 128))
    return lax.all_to_all(same, axis, 0, 0, tiled=True).reshape(size * rows, 128)


def on_device(
    rhs, coords, basis, lt, dt, t1, t2, t3, far_list, far_count, far_coupling, top_list, top_coupling,
    near_list,
):
    dev = lax.axis_index(DEV).astype(jnp.int32).reshape(1)
    tie = lax.optimization_barrier
    payload, own = up_pass(dev, rhs, coords, basis, lt, dt)
    blocks = lax.all_to_all(payload, ("zh", "zl"), 0, 0, tiled=True).reshape(256, 128)
    swap_a = lax.ppermute(own, DEV, [(i, i ^ 1) for i in range(512)])
    swap_b = lax.ppermute(own, DEV, [(i, ((i + 1) ^ 1) - 1) for i in range(1, 511)] + [(0, 511), (511, 0)])
    own, t1 = tie((own, t1))
    dev_a = order_pass(dev, t1)
    blocks, swap_a, swap_b, dev_a = tie((blocks, swap_a, swap_b, dev_a))
    near_list = jnp.transpose(near_list)
    gathered = spread(blocks, ("x", "y"), 16)
    near_a, packed, path = near_and_prep(
        dev_a, near_list, swap_a, own, swap_b, t1, t2, t3, far_coupling, top_coupling, 0, 12
    )
    gathered, near_a, packed = tie((gathered, near_a, packed))
    other = cyclic(gathered, "core", 2, 1)
    sums, packed = half_pass(gathered, packed)
    shares = mid_pass(dev, far_list, far_count, top_list, gathered, other, sums, packed)
    shares, dev_b = tie((shares, dev))
    near_b = near_field(dev_b, near_list, swap_a, own, swap_b, 12, 16)
    shares = lax.all_to_all(shares, ("zl", "core"), 0, 0, tiled=True)
    return down_pass(dev, shares, path, dt, lt, basis, (near_a, near_b))


def solution(mesh):
    torus = Mesh(mesh.devices.reshape(4, 4, 4, 2, 4), DEV)
    branch = DEV[:4]
    in_specs = (
        P(None, DEV),
        P(None, DEV),
        P(DEV, None, None),
        P(DEV, None, None),
        P(DEV, None, None),
        P(),
        P(),
        P(),
        P(DEV, None),
        P(DEV),
        P(DEV, None, None, None),
        P(branch, None, None),
        P(branch, None, None, None, None),
        P(DEV, None),
    )
    return jax.shard_map(
        on_device, mesh=torus, in_specs=in_specs, out_specs=P(None, DEV), check_vma=False
    )
```

```python
import functools

import jax
import jax.numpy as jnp
import numpy as np
from jax import lax
from jax.experimental import pallas as pl
from jax.experimental.pallas import tpu as pltpu
from jax.sharding import Mesh, PartitionSpec as P

F32 = jnp.float32
BF16 = jnp.bfloat16
DEV = ("x", "zh", "zl", "core", "y")
SCALE = float(20.0 * np.log2(np.e))
NT = (((1,), (1,)), ((), ()))
NN = (((1,), (0,)), ((), ()))
GRANT = 60 * 1024 * 1024
PACKED = 10240
ROOM = 98304


def dot(a, b, dims):
    return lax.dot_general(a, b, dims, preferred_element_type=F32)


def split(v):
    hi = v.astype(BF16)
    lo = (v - hi.astype(F32)).astype(BF16)
    return hi, lo


def wide_dot(v, b, dims):
    rows = v.shape[0]
    hi, lo = split(v)
    out = dot(jnp.concatenate([hi, lo], axis=0), b, dims)
    return out[:rows] + out[rows:]


def vmem(n):
    return [pl.BlockSpec(memory_space=pltpu.VMEM)] * n


def hbm(n):
    return [pl.BlockSpec(memory_space=pltpu.HBM)] * n


def smem(n):
    return [pl.BlockSpec(memory_space=pltpu.SMEM)] * n


def copies(sources, targets, sems):
    return [
        pltpu.make_async_copy(source, target, sems.at[k])
        for k, (source, target) in enumerate(zip(sources, targets))
    ]


def up_kernel(
    id_ref, rhs_hbm, coords_hbm, basis_hbm, lt_hbm, dt_hbm,
    out_ref, own_ref, rhs_ref, coords_ref, basis_ref, lt_ref, dt_ref, sems,
):
    moves = copies(
        (rhs_hbm, coords_hbm, basis_hbm, lt_hbm, dt_hbm),
        (rhs_ref, coords_ref, basis_ref, lt_ref, dt_ref),
        sems,
    )
    for move in moves:
        move.start()
    for move in moves:
        move.wait()
    total = jnp.zeros((16, 64), F32)
    for leaf in range(16):
        coeffs = dot(rhs_ref[:, leaf * 256 : (leaf + 1) * 256], basis_ref[leaf], NT)
        total = total + wide_dot(coeffs, lt_ref[leaf], NT)
    lifted = wide_dot(total, dt_ref[0], NT)
    even = (id_ref[0] >> 2) & 1 == 0
    first = jnp.where(even, lifted, total)
    second = jnp.where(even, total, lifted)
    both = jnp.concatenate([first, second], axis=1).astype(BF16)
    for k in range(16):
        out_ref[k] = both
    own_ref[0:16, :] = rhs_ref[...]
    xyz = coords_ref[...].astype(F32)
    own_ref[16:24, :] = jnp.concatenate([xyz, jnp.zeros((5, 4096), F32)], axis=0).astype(BF16)


def up_pass(dev, rhs, coords, basis, lt, dt):
    return pl.pallas_call(
        up_kernel,
        out_shape=[
            jax.ShapeDtypeStruct((16, 16, 128), BF16),
            jax.ShapeDtypeStruct((24, 4096), BF16),
        ],
        in_specs=smem(1) + hbm(5),
        out_specs=vmem(2),
        scratch_shapes=[
            pltpu.VMEM((16, 4096), BF16),
            pltpu.VMEM((3, 4096), BF16),
            pltpu.VMEM((16, 64, 256), BF16),
            pltpu.VMEM((16, 64, 64), BF16),
            pltpu.VMEM((1, 64, 64), BF16),
            pltpu.SemaphoreType.DMA((5,)),
        ],
        compiler_params=pltpu.CompilerParams(vmem_limit_bytes=GRANT),
        cost_estimate=pl.CostEstimate(flops=20_000_000, bytes_accessed=1_000_000, transcendentals=0),
        name="up_pass",
    )(dev, rhs, coords, basis, lt, dt)


def prepare(
    id_ref, t1_ref, t2_ref, t3_ref, fc_ref, tc_ref, packed_ref, path_ref
):
    def put(at, first, second):
        packed_ref[at * 64 : (at + 1) * 64, :] = jnp.concatenate([first, second], axis=1)

    for source, offset, nodes in ((t1_ref, 0, 64), (t2_ref, 64, 32), (t3_ref, 96, 16)):
        for n in range(nodes):
            put(offset + n, source[2 * n], source[2 * n + 1])
    for slot in range(16):
        put(112 + slot, fc_ref[0, slot], fc_ref[0, slot])
    for level in range(4):
        for slot in range(8):
            put(128 + level * 8 + slot, tc_ref[0, level, slot], tc_ref[0, level, slot])
    branch = id_ref[0] >> 2
    path_ref[0] = t1_ref[branch]
    path_ref[1] = t2_ref[branch >> 1]
    path_ref[2] = t3_ref[branch >> 2]


def order_kernel(id_ref, t1_hbm, out_ref):
    out_ref[0] = id_ref[0]


def order_pass(dev, t1):
    return pl.pallas_call(
        order_kernel,
        out_shape=jax.ShapeDtypeStruct((1,), jnp.int32),
        in_specs=smem(1) + hbm(1),
        out_specs=smem(1)[0],
        compiler_params=pltpu.CompilerParams(vmem_limit_bytes=GRANT),
        cost_estimate=pl.CostEstimate(flops=0, bytes_accessed=64, transcendentals=0),
        name="order_pass",
    )(dev, t1)


def features(xyz, centre):
    moved = (xyz - centre) * SCALE
    hi, lo = split(moved)
    exact = hi.astype(F32) + lo.astype(F32)
    norm = jnp.sum(exact * exact, axis=0, keepdims=True)
    n1 = norm.astype(BF16).astype(F32)
    n2 = (norm - n1).astype(BF16).astype(F32)
    n3 = norm - n1 - n2
    row = lax.broadcasted_iota(jnp.int32, xyz.shape, 0)
    norms = jnp.where(row == 0, n1, jnp.where(row == 1, n2, jnp.where(row == 2, n3, 0.0)))
    ones = jnp.where(row < 3, 1.0, 0.0)
    return hi.astype(F32), lo.astype(F32), norms, ones


def near_kernel(
    first, last, id_ref, near_ref, swap_a_ref, own_ref, swap_b_ref, out_ref, feat, rhs, target, between=None
):
    own_xyz = own_ref[16:24, :].astype(F32)
    low = jnp.min(own_xyz, axis=1, keepdims=True)
    high = jnp.max(own_xyz, axis=1, keepdims=True)
    centre = 0.5 * (low + high)
    for part, ref in enumerate((swap_a_ref, own_ref, swap_b_ref)):
        cols = pl.ds(part * 4096, 4096)
        rhs[:, cols] = ref[0:16, :]
        xyz = ref[16:24, :].astype(F32)
        hi, lo, norms, ones = features(xyz, centre)
        both = jnp.concatenate([hi, lo], axis=0).astype(BF16)
        feat[0:16, cols] = both
        feat[16:32, cols] = both
        feat[32:48, cols] = jnp.concatenate([ones, norms], axis=0).astype(BF16)
        if part == 1:
            for leaf in range(first, last):
                c = slice(leaf * 256, (leaf + 1) * 256)
                h = -2.0 * hi[:, c]
                m = -2.0 * lo[:, c]
                stack = jnp.concatenate([h, h, m, m, norms[:, c], ones[:, c]], axis=0)
                target[leaf - first] = jnp.transpose(stack).astype(BF16)
    if between is not None:
        between()
    base = (id_ref[0] - 1) * 16
    even = (id_ref[0] & 1) == 0

    def leaf_step(step, carry):
        left = target[step]
        total = jnp.zeros((16, 256), F32)
        for slot in range(8):
            source = near_ref[slot, first + step] - base
            source = jnp.minimum(jnp.maximum(source, 0), 47)
            part = source >> 4
            source = jnp.where(even, 2 - part, part) * 16 + (source & 15)
            cols = pl.ds(pl.multiple_of(source * 256, 256), 256)
            squared = jnp.maximum(dot(left, feat[:, cols], NN), 1e-20)
            tile = jnp.exp2(-(squared * lax.rsqrt(squared))).astype(BF16)
            total = total + dot(rhs[:, cols], tile, NT)
        out_ref[:, pl.ds(pl.multiple_of(step * 256, 256), 256)] = total
        return carry

    lax.fori_loop(0, last - first, leaf_step, 0, unroll=4)


def near_and_prep_kernel(
    first, last, id_ref, near_ref, swap_a_ref, own_ref, swap_b_ref, t1_hbm, t2_hbm, t3_hbm, fc_hbm, tc_hbm,
    out_ref, packed_hbm, path_ref,
    feat, rhs, target, packed, t1_ref, t2_ref, t3_ref, fc_ref, tc_ref, sems,
):
    moves = copies((t1_hbm, t2_hbm, t3_hbm, fc_hbm, tc_hbm), (t1_ref, t2_ref, t3_ref, fc_ref, tc_ref), sems)
    out = pltpu.make_async_copy(packed, packed_hbm.at[0:PACKED, :], sems.at[5])
    for move in moves:
        move.start()

    def between():
        for move in moves:
            move.wait()
        prepare(id_ref, t1_ref, t2_ref, t3_ref, fc_ref, tc_ref, packed, path_ref)
        out.start()

    near_kernel(
        first, last, id_ref, near_ref, swap_a_ref, own_ref, swap_b_ref, out_ref, feat, rhs, target, between
    )
    out.wait()


def near_cost(leaves):
    return pl.CostEstimate(
        flops=400_000_000 * leaves, bytes_accessed=600_000, transcendentals=1_050_000 * leaves
    )


def near_scratch(leaves):
    return [
        pltpu.VMEM((48, 12288), BF16),
        pltpu.VMEM((16, 12288), BF16),
        pltpu.VMEM((leaves, 256, 48), BF16),
    ]


def near_and_prep(dev, near_list, swap_a, own, swap_b, t1, t2, t3, fc, tc, first, last):
    return pl.pallas_call(
        functools.partial(near_and_prep_kernel, first, last),
        out_shape=[
            jax.ShapeDtypeStruct((16, (last - first) * 256), F32),
            jax.ShapeDtypeStruct((ROOM, 128), BF16),
            jax.ShapeDtypeStruct((3, 64, 64), BF16),
        ],
        in_specs=smem(2) + vmem(3) + hbm(5),
        out_specs=vmem(1) + hbm(1) + vmem(1),
        scratch_shapes=near_scratch(last - first)
        + [
            pltpu.VMEM((PACKED, 128), BF16),
            pltpu.VMEM((128, 64, 64), BF16),
            pltpu.VMEM((64, 64, 64), BF16),
            pltpu.VMEM((32, 64, 64), BF16),
            pltpu.VMEM((1, 16, 64, 64), BF16),
            pltpu.VMEM((1, 4, 8, 64, 64), BF16),
            pltpu.SemaphoreType.DMA((6,)),
        ],
        compiler_params=pltpu.CompilerParams(vmem_limit_bytes=GRANT),
        cost_estimate=near_cost(last - first + 2),
        name="near_and_prep",
    )(dev, near_list, swap_a, own, swap_b, t1, t2, t3, fc, tc)


def near_field(dev, near_list, swap_a, own, swap_b, first, last):
    return pl.pallas_call(
        functools.partial(near_kernel, first, last),
        out_shape=jax.ShapeDtypeStruct((16, (last - first) * 256), F32),
        in_specs=smem(2) + vmem(3),
        out_specs=vmem(1)[0],
        scratch_shapes=near_scratch(last - first),
        compiler_params=pltpu.CompilerParams(vmem_limit_bytes=GRANT),
        cost_estimate=near_cost(last - first + 1),
        name="near_field",
    )(dev, near_list, swap_a, own, swap_b)


def half_kernel(own_ref, packed_hbm, sums_ref, packed_ref, sem):
    move = pltpu.make_async_copy(packed_hbm.at[0:PACKED, :], packed_ref, sem)
    move.start()
    for x in range(4):
        parts = [own_ref[(x * 4 + y) * 256 : (x * 4 + y + 1) * 256, :].astype(F32) for y in range(4)]
        sums_ref[x * 256 : (x + 1) * 256, :] = (parts[0] + parts[1]) + (parts[2] + parts[3])
    move.wait()


def half_pass(own, packed):
    return pl.pallas_call(
        half_kernel,
        out_shape=[
            jax.ShapeDtypeStruct((1024, 128), F32),
            jax.ShapeDtypeStruct((PACKED, 128), BF16),
        ],
        in_specs=vmem(1) + hbm(1),
        out_specs=vmem(2),
        scratch_shapes=[pltpu.SemaphoreType.DMA],
        compiler_params=pltpu.CompilerParams(vmem_limit_bytes=GRANT - 16 * 1024 * 1024),
        cost_estimate=pl.CostEstimate(flops=1_000_000, bytes_accessed=5_000_000, transcendentals=0),
        name="half_pass",
    )(own, packed)


def mid_kernel(
    id_ref, flist_ref, fcount_ref, tlist_ref, own_ref, other_ref, sums_ref, packed,
    shares_ref, nodes,
):
    my_core = (id_ref[0] >> 2) & 1
    lane16 = lax.broadcasted_iota(jnp.int32, (16, 128), 1)
    low16 = lane16 < 64
    half16 = jnp.where(low16, 0, 1)
    from_own = half16 == my_core

    def put(at, value):
        hi, lo = split(value)
        nodes[at] = jnp.concatenate([hi, lo], axis=0)

    def raise_four(pairs, weights):
        value = jnp.concatenate(pairs, axis=0)
        hi, lo = split(value)
        out = dot(jnp.concatenate([hi, lo], axis=0), weights, NT)
        out = out[:64] + out[64:]
        first = jnp.where(low16, out[0:16, 0:128], out[16:32, 0:128])
        second = jnp.where(low16, out[32:48, 128:256], out[48:64, 128:256])
        return first, second

    def side_by_side(first, count):
        return jnp.concatenate([packed[(first + k) * 64 : (first + k + 1) * 64, :] for k in range(count)], axis=1)

    ones = []
    for at_x in range(4):
        for z in range(16):
            at = (at_x * 64 + z) * 16
            parts = [other_ref[y * 256 + at : y * 256 + at + 16, :].astype(F32) for y in range(4)]
            other = (parts[0] + parts[1]) + (parts[2] + parts[3])
            row = (at_x * 16 + z) * 16
            ones.append(jnp.where(from_own, sums_ref[row : row + 16, :], other))
            put(at_x * 16 + z, ones[-1])
    for at_x in range(4):
        twos = []
        for quad in range(4):
            node = at_x * 16 + quad * 4
            twos.extend(raise_four(ones[node : node + 4], packed[node * 64 : node * 64 + 256, :]))
        for k in range(8):
            put(64 + at_x * 8 + k, twos[k])
        threes = []
        for quad in range(2):
            row = (64 + at_x * 8 + quad * 4) * 64
            threes.extend(raise_four(twos[quad * 4 : quad * 4 + 4], packed[row : row + 256, :]))
        for k in range(4):
            put(96 + at_x * 4 + k, threes[k])
        row = (96 + at_x * 4) * 64
        fours = raise_four(threes, packed[row : row + 256, :])
        for k in range(2):
            put(112 + at_x * 2 + k, fours[k])

    blocks = []
    for slot in range(16):
        c = flist_ref[0, slot]
        c_y, c_core = c & 3, (c >> 2) & 1
        place = pl.multiple_of((((c >> 7) * 4 + c_y) * 16 + ((c >> 3) & 15)) * 16, 16)
        block = jnp.where(c_core == my_core, own_ref[pl.ds(place, 16), :], other_ref[pl.ds(place, 16), :])
        live = jnp.where(slot < fcount_ref[0], 1 - c_core, 2)
        blocks.append(block * jnp.where(half16 == live, 1.0, 0.0).astype(BF16))
    far = dot(jnp.concatenate(blocks, axis=1), side_by_side(112, 16), NT)

    parts = []
    for level, offset in enumerate((0, 64, 96, 112)):
        blocks = []
        for slot in range(8):
            node = tlist_ref[0, level, slot]
            block = nodes[offset + (node >> 1)]
            mask = jnp.where(half16 == (node & 1), 1.0, 0.0).astype(BF16)
            blocks.append(block * jnp.concatenate([mask, mask], axis=0))
        out = dot(jnp.concatenate(blocks, axis=1), side_by_side(128 + level * 8, 8), NT)
        parts.append(out[:16] + out[16:])
    upper = jnp.concatenate([parts[1], parts[2]], axis=1)
    last = jnp.concatenate([parts[3], parts[0]], axis=1)
    far = jnp.concatenate([far, far], axis=1)
    packed_shares = jnp.concatenate([upper, last, far], axis=0).astype(BF16)
    for k in range(8):
        shares_ref[k] = packed_shares


def mid_pass(dev, flist, fcount, tlist, own, other, sums, packed):
    return pl.pallas_call(
        mid_kernel,
        out_shape=jax.ShapeDtypeStruct((8, 48, 128), BF16),
        in_specs=smem(4) + vmem(4),
        out_specs=vmem(1)[0],
        scratch_shapes=[pltpu.VMEM((120, 32, 128), BF16)],
        compiler_params=pltpu.CompilerParams(vmem_limit_bytes=GRANT - 16 * 1024 * 1024),
        cost_estimate=pl.CostEstimate(flops=300_000_000, bytes_accessed=5_000_000, transcendentals=0),
        name="mid_pass",
    )(dev, flist, fcount, tlist, own, other, sums, packed)


def down_kernel(
    id_ref, shares_hbm, path_hbm, dt_hbm, lt_hbm, basis_hbm, near_a_hbm, near_b_hbm,
    out_ref, shares_ref, path_ref, dt_ref, lt_ref, basis_ref, near_a, near_b, sems,
):
    moves = copies(
        (shares_hbm, path_hbm, dt_hbm, lt_hbm, basis_hbm, near_a_hbm, near_b_hbm),
        (shares_ref, path_ref, dt_ref, lt_ref, basis_ref, near_a, near_b),
        sems,
    )
    for move in moves:
        move.start()
    for move in moves[:3]:
        move.wait()
    zl = (id_ref[0] >> 3) & 3
    mine = shares_ref[(id_ref[0] >> 2) & 7].astype(F32)
    upper = jnp.zeros((16, 128), F32)
    down = jnp.zeros((16, 64), F32)
    low = lax.broadcasted_iota(jnp.int32, (16, 128), 1) < 64
    for o in range(8):
        pair = jnp.where((o >> 1) == zl, 1.0, 0.0)
        quad = jnp.where((o >> 2) == (zl >> 1), 1.0, 0.0)
        share = shares_ref[o].astype(F32)
        upper = upper + share[0:16, :] * jnp.where(low, pair, quad)
        down = down + share[16:32, 0:64]
    down = upper[:, 64:128] + wide_dot(down, path_ref[2], NN)
    down = upper[:, 0:64] + wide_dot(down, path_ref[1], NN)
    down = mine[16:32, 64:128] + wide_dot(down, path_ref[0], NN)
    down = mine[32:48, 0:64] + wide_dot(down, dt_ref[0], NN)
    for move in moves[3:]:
        move.wait()
    near_refs = (near_a, near_b)
    near_blocks = [(ref, k) for ref in near_refs for k in range(ref.shape[1] // 256)]
    for leaf in range(16):
        near_ref, k = near_blocks[leaf]
        leaf_down = wide_dot(down, lt_ref[leaf], NN).astype(BF16)
        cols = slice(leaf * 256, (leaf + 1) * 256)
        near = near_ref[:, k * 256 : (k + 1) * 256]
        out_ref[:, cols] = near + dot(leaf_down, basis_ref[leaf], NN)


def down_pass(dev, shares, path, dt, lt, basis, near):
    return pl.pallas_call(
        down_kernel,
        out_shape=jax.ShapeDtypeStruct((16, 4096), F32),
        in_specs=smem(1) + hbm(7),
        out_specs=vmem(1)[0],
        scratch_shapes=[
            pltpu.VMEM((8, 48, 128), BF16),
            pltpu.VMEM((3, 64, 64), BF16),
            pltpu.VMEM((1, 64, 64), BF16),
            pltpu.VMEM((16, 64, 64), BF16),
            pltpu.VMEM((16, 64, 256), BF16),
            pltpu.VMEM(near[0].shape, F32),
            pltpu.VMEM(near[1].shape, F32),
            pltpu.SemaphoreType.DMA((7,)),
        ],
        compiler_params=pltpu.CompilerParams(vmem_limit_bytes=GRANT),
        cost_estimate=pl.CostEstimate(flops=20_000_000, bytes_accessed=1_500_000, transcendentals=0),
        name="down_pass",
    )(dev, shares, path, dt, lt, basis, *near)


def cyclic(value, axis, size, by):
    return lax.ppermute(value, axis, [(i, (i + by) % size) for i in range(size)])


def spread(value, axis, size):
    rows = value.shape[0]
    same = jnp.broadcast_to(value[None], (size, rows, 128))
    return lax.all_to_all(same, axis, 0, 0, tiled=True).reshape(size * rows, 128)


def on_device(
    rhs, coords, basis, lt, dt, t1, t2, t3, far_list, far_count, far_coupling, top_list, top_coupling,
    near_list,
):
    dev = lax.axis_index(DEV).astype(jnp.int32).reshape(1)
    tie = lax.optimization_barrier
    payload, own = up_pass(dev, rhs, coords, basis, lt, dt)
    blocks = lax.all_to_all(payload, ("zh", "zl"), 0, 0, tiled=True).reshape(256, 128)
    swap_a = lax.ppermute(own, DEV, [(i, i ^ 1) for i in range(512)])
    swap_b = lax.ppermute(own, DEV, [(i, ((i + 1) ^ 1) - 1) for i in range(1, 511)] + [(0, 511), (511, 0)])
    own, t1 = tie((own, t1))
    dev_a = order_pass(dev, t1)
    blocks, swap_a, swap_b, dev_a = tie((blocks, swap_a, swap_b, dev_a))
    near_list = jnp.transpose(near_list)
    gathered = spread(blocks, ("x", "y"), 16)
    near_a, packed, path = near_and_prep(
        dev_a, near_list, swap_a, own, swap_b, t1, t2, t3, far_coupling, top_coupling, 0, 12
    )
    gathered, near_a, packed = tie((gathered, near_a, packed))
    other = cyclic(gathered, "core", 2, 1)
    sums, packed = half_pass(gathered, packed)
    shares = mid_pass(dev, far_list, far_count, top_list, gathered, other, sums, packed)
    shares, dev_b = tie((shares, dev))
    near_b = near_field(dev_b, near_list, swap_a, own, swap_b, 12, 16)
    shares = lax.all_to_all(shares, ("zl", "core"), 0, 0, tiled=True)
    return down_pass(dev, shares, path, dt, lt, basis, (near_a, near_b))


def solution(mesh):
    torus = Mesh(mesh.devices.reshape(4, 4, 4, 2, 4), DEV)
    branch = DEV[:4]
    in_specs = (
        P(None, DEV),
        P(None, DEV),
        P(DEV, None, None),
        P(DEV, None, None),
        P(DEV, None, None),
        P(),
        P(),
        P(),
        P(DEV, None),
        P(DEV),
        P(DEV, None, None, None),
        P(branch, None, None),
        P(branch, None, None, None, None),
        P(DEV, None),
    )
    return jax.shard_map(
        on_device, mesh=torus, in_specs=in_specs, out_specs=P(None, DEV), check_vma=False
    )
```

```python
import functools

import jax
import jax.numpy as jnp
import numpy as np
from jax import lax
from jax.experimental import pallas as pl
from jax.experimental.pallas import tpu as pltpu
from jax.sharding import Mesh, PartitionSpec as P

F32 = jnp.float32
BF16 = jnp.bfloat16
DEV = ("x", "zh", "zl", "core", "y")
SCALE = float(20.0 * np.log2(np.e))
NT = (((1,), (1,)), ((), ()))
NN = (((1,), (0,)), ((), ()))
GRANT = 60 * 1024 * 1024
PACKED = 10240
ROOM = 98304


def dot(a, b, dims):
    return lax.dot_general(a, b, dims, preferred_element_type=F32)


def split(v):
    hi = v.astype(BF16)
    lo = (v - hi.astype(F32)).astype(BF16)
    return hi, lo


def wide_dot(v, b, dims):
    rows = v.shape[0]
    hi, lo = split(v)
    out = dot(jnp.concatenate([hi, lo], axis=0), b, dims)
    return out[:rows] + out[rows:]


def vmem(n):
    return [pl.BlockSpec(memory_space=pltpu.VMEM)] * n


def hbm(n):
    return [pl.BlockSpec(memory_space=pltpu.HBM)] * n


def smem(n):
    return [pl.BlockSpec(memory_space=pltpu.SMEM)] * n


def copies(sources, targets, sems):
    return [
        pltpu.make_async_copy(source, target, sems.at[k])
        for k, (source, target) in enumerate(zip(sources, targets))
    ]


def up_kernel(
    id_ref, rhs_hbm, coords_hbm, basis_hbm, lt_hbm, dt_hbm,
    out_ref, own_ref, rhs_ref, coords_ref, basis_ref, lt_ref, dt_ref, sems,
):
    moves = copies(
        (rhs_hbm, coords_hbm, basis_hbm, lt_hbm, dt_hbm),
        (rhs_ref, coords_ref, basis_ref, lt_ref, dt_ref),
        sems,
    )
    for move in moves:
        move.start()
    for move in moves:
        move.wait()
    total = jnp.zeros((16, 64), F32)
    for leaf in range(16):
        coeffs = dot(rhs_ref[:, leaf * 256 : (leaf + 1) * 256], basis_ref[leaf], NT)
        total = total + wide_dot(coeffs, lt_ref[leaf], NT)
    lifted = wide_dot(total, dt_ref[0], NT)
    even = (id_ref[0] >> 2) & 1 == 0
    first = jnp.where(even, lifted, total)
    second = jnp.where(even, total, lifted)
    both = jnp.concatenate([first, second], axis=1).astype(BF16)
    for k in range(16):
        out_ref[k] = both
    own_ref[0:16, :] = rhs_ref[...]
    xyz = coords_ref[...].astype(F32)
    own_ref[16:24, :] = jnp.concatenate([xyz, jnp.zeros((5, 4096), F32)], axis=0).astype(BF16)


def up_pass(dev, rhs, coords, basis, lt, dt):
    return pl.pallas_call(
        up_kernel,
        out_shape=[
            jax.ShapeDtypeStruct((16, 16, 128), BF16),
            jax.ShapeDtypeStruct((24, 4096), BF16),
        ],
        in_specs=smem(1) + hbm(5),
        out_specs=vmem(2),
        scratch_shapes=[
            pltpu.VMEM((16, 4096), BF16),
            pltpu.VMEM((3, 4096), BF16),
            pltpu.VMEM((16, 64, 256), BF16),
            pltpu.VMEM((16, 64, 64), BF16),
            pltpu.VMEM((1, 64, 64), BF16),
            pltpu.SemaphoreType.DMA((5,)),
        ],
        compiler_params=pltpu.CompilerParams(vmem_limit_bytes=GRANT),
        cost_estimate=pl.CostEstimate(flops=20_000_000, bytes_accessed=1_000_000, transcendentals=0),
        name="up_pass",
    )(dev, rhs, coords, basis, lt, dt)


def prepare(
    id_ref, t1_ref, t2_ref, t3_ref, fc_ref, tc_ref, packed_ref, path_ref
):
    def put(at, first, second):
        packed_ref[at * 64 : (at + 1) * 64, :] = jnp.concatenate([first, second], axis=1)

    for source, offset, nodes in ((t1_ref, 0, 64), (t2_ref, 64, 32), (t3_ref, 96, 16)):
        for n in range(nodes):
            put(offset + n, source[2 * n], source[2 * n + 1])
    for slot in range(16):
        put(112 + slot, fc_ref[0, slot], fc_ref[0, slot])
    for level in range(4):
        for slot in range(8):
            put(128 + level * 8 + slot, tc_ref[0, level, slot], tc_ref[0, level, slot])
    branch = id_ref[0] >> 2
    path_ref[0] = t1_ref[branch]
    path_ref[1] = t2_ref[branch >> 1]
    path_ref[2] = t3_ref[branch >> 2]


def order_kernel(id_ref, t1_hbm, out_ref):
    out_ref[0] = id_ref[0]


def order_pass(dev, t1):
    return pl.pallas_call(
        order_kernel,
        out_shape=jax.ShapeDtypeStruct((1,), jnp.int32),
        in_specs=smem(1) + hbm(1),
        out_specs=smem(1)[0],
        compiler_params=pltpu.CompilerParams(vmem_limit_bytes=GRANT),
        cost_estimate=pl.CostEstimate(flops=0, bytes_accessed=64, transcendentals=0),
        name="order_pass",
    )(dev, t1)


def features(xyz, centre):
    moved = (xyz - centre) * SCALE
    hi, lo = split(moved)
    exact = hi.astype(F32) + lo.astype(F32)
    norm = jnp.sum(exact * exact, axis=0, keepdims=True)
    n1 = norm.astype(BF16).astype(F32)
    n2 = (norm - n1).astype(BF16).astype(F32)
    n3 = norm - n1 - n2
    row = lax.broadcasted_iota(jnp.int32, xyz.shape, 0)
    norms = jnp.where(row == 0, n1, jnp.where(row == 1, n2, jnp.where(row == 2, n3, 0.0)))
    ones = jnp.where(row < 3, 1.0, 0.0)
    return hi.astype(F32), lo.astype(F32), norms, ones


def near_kernel(
    first, last, id_ref, near_ref, swap_a_ref, own_ref, swap_b_ref, out_ref, feat, rhs, target, between=None
):
    own_xyz = own_ref[16:24, :].astype(F32)
    low = jnp.min(own_xyz, axis=1, keepdims=True)
    high = jnp.max(own_xyz, axis=1, keepdims=True)
    centre = 0.5 * (low + high)
    for part, ref in enumerate((swap_a_ref, own_ref, swap_b_ref)):
        cols = pl.ds(part * 4096, 4096)
        rhs[:, cols] = ref[0:16, :]
        xyz = ref[16:24, :].astype(F32)
        hi, lo, norms, ones = features(xyz, centre)
        both = jnp.concatenate([hi, lo], axis=0).astype(BF16)
        feat[0:16, cols] = both
        feat[16:32, cols] = both
        feat[32:48, cols] = jnp.concatenate([ones, norms], axis=0).astype(BF16)
        if part == 1:
            for leaf in range(first, last):
                c = slice(leaf * 256, (leaf + 1) * 256)
                h = -2.0 * hi[:, c]
                m = -2.0 * lo[:, c]
                stack = jnp.concatenate([h, h, m, m, norms[:, c], ones[:, c]], axis=0)
                target[leaf - first] = jnp.transpose(stack).astype(BF16)
    if between is not None:
        between()
    base = (id_ref[0] - 1) * 16
    even = (id_ref[0] & 1) == 0

    def leaf_step(step, carry):
        left = target[step]
        total = jnp.zeros((16, 256), F32)
        for slot in range(8):
            source = near_ref[slot, first + step] - base
            source = jnp.minimum(jnp.maximum(source, 0), 47)
            part = source >> 4
            source = jnp.where(even, 2 - part, part) * 16 + (source & 15)
            cols = pl.ds(pl.multiple_of(source * 256, 256), 256)
            squared = jnp.maximum(dot(left, feat[:, cols], NN), 1e-20)
            tile = jnp.exp2(-(squared * lax.rsqrt(squared))).astype(BF16)
            total = total + dot(rhs[:, cols], tile, NT)
        out_ref[:, pl.ds(pl.multiple_of(step * 256, 256), 256)] = total
        return carry

    lax.fori_loop(0, last - first, leaf_step, 0, unroll=4)


def near_and_prep_kernel(
    first, last, id_ref, near_ref, swap_a_ref, own_ref, swap_b_ref, t1_hbm, t2_hbm, t3_hbm, fc_hbm, tc_hbm,
    out_ref, packed_hbm, path_ref,
    feat, rhs, target, packed, t1_ref, t2_ref, t3_ref, fc_ref, tc_ref, sems,
):
    moves = copies((t1_hbm, t2_hbm, t3_hbm, fc_hbm, tc_hbm), (t1_ref, t2_ref, t3_ref, fc_ref, tc_ref), sems)
    out = pltpu.make_async_copy(packed, packed_hbm.at[0:PACKED, :], sems.at[5])
    for move in moves:
        move.start()

    def between():
        for move in moves:
            move.wait()
        prepare(id_ref, t1_ref, t2_ref, t3_ref, fc_ref, tc_ref, packed, path_ref)
        out.start()

    near_kernel(
        first, last, id_ref, near_ref, swap_a_ref, own_ref, swap_b_ref, out_ref, feat, rhs, target, between
    )
    out.wait()


def near_cost(leaves):
    return pl.CostEstimate(
        flops=400_000_000 * leaves, bytes_accessed=600_000, transcendentals=1_050_000 * leaves
    )


def near_scratch(leaves):
    return [
        pltpu.VMEM((48, 12288), BF16),
        pltpu.VMEM((16, 12288), BF16),
        pltpu.VMEM((leaves, 256, 48), BF16),
    ]


def near_and_prep(dev, near_list, swap_a, own, swap_b, t1, t2, t3, fc, tc, first, last):
    return pl.pallas_call(
        functools.partial(near_and_prep_kernel, first, last),
        out_shape=[
            jax.ShapeDtypeStruct((16, (last - first) * 256), F32),
            jax.ShapeDtypeStruct((ROOM, 128), BF16),
            jax.ShapeDtypeStruct((3, 64, 64), BF16),
        ],
        in_specs=smem(2) + vmem(3) + hbm(5),
        out_specs=vmem(1) + hbm(1) + vmem(1),
        scratch_shapes=near_scratch(last - first)
        + [
            pltpu.VMEM((PACKED, 128), BF16),
            pltpu.VMEM((128, 64, 64), BF16),
            pltpu.VMEM((64, 64, 64), BF16),
            pltpu.VMEM((32, 64, 64), BF16),
            pltpu.VMEM((1, 16, 64, 64), BF16),
            pltpu.VMEM((1, 4, 8, 64, 64), BF16),
            pltpu.SemaphoreType.DMA((6,)),
        ],
        compiler_params=pltpu.CompilerParams(vmem_limit_bytes=GRANT),
        cost_estimate=near_cost(last - first + 2),
        name="near_and_prep",
    )(dev, near_list, swap_a, own, swap_b, t1, t2, t3, fc, tc)


def near_field(dev, near_list, swap_a, own, swap_b, first, last):
    return pl.pallas_call(
        functools.partial(near_kernel, first, last),
        out_shape=jax.ShapeDtypeStruct((16, (last - first) * 256), F32),
        in_specs=smem(2) + vmem(3),
        out_specs=vmem(1)[0],
        scratch_shapes=near_scratch(last - first),
        compiler_params=pltpu.CompilerParams(vmem_limit_bytes=GRANT),
        cost_estimate=near_cost(last - first + 1),
        name="near_field",
    )(dev, near_list, swap_a, own, swap_b)


def half_kernel(own_ref, packed_hbm, sums_ref, packed_ref, sem):
    move = pltpu.make_async_copy(packed_hbm.at[0:PACKED, :], packed_ref, sem)
    move.start()
    for x in range(4):
        parts = [own_ref[(x * 4 + y) * 256 : (x * 4 + y + 1) * 256, :].astype(F32) for y in range(4)]
        sums_ref[x * 256 : (x + 1) * 256, :] = (parts[0] + parts[1]) + (parts[2] + parts[3])
    move.wait()


def half_pass(own, packed):
    return pl.pallas_call(
        half_kernel,
        out_shape=[
            jax.ShapeDtypeStruct((1024, 128), F32),
            jax.ShapeDtypeStruct((PACKED, 128), BF16),
        ],
        in_specs=vmem(1) + hbm(1),
        out_specs=vmem(2),
        scratch_shapes=[pltpu.SemaphoreType.DMA],
        compiler_params=pltpu.CompilerParams(vmem_limit_bytes=GRANT - 16 * 1024 * 1024),
        cost_estimate=pl.CostEstimate(flops=1_000_000, bytes_accessed=5_000_000, transcendentals=0),
        name="half_pass",
    )(own, packed)


def mid_kernel(
    id_ref, flist_ref, fcount_ref, tlist_ref, own_ref, other_ref, sums_ref, packed,
    shares_ref, nodes,
):
    my_core = (id_ref[0] >> 2) & 1
    lane16 = lax.broadcasted_iota(jnp.int32, (16, 128), 1)
    low16 = lane16 < 64
    half16 = jnp.where(low16, 0, 1)
    from_own = half16 == my_core

    def put(at, value):
        hi, lo = split(value)
        nodes[at] = jnp.concatenate([hi, lo], axis=0)

    def raise_four(pairs, weights):
        value = jnp.concatenate(pairs, axis=0)
        hi, lo = split(value)
        out = dot(jnp.concatenate([hi, lo], axis=0), weights, NT)
        out = out[:64] + out[64:]
        first = jnp.where(low16, out[0:16, 0:128], out[16:32, 0:128])
        second = jnp.where(low16, out[32:48, 128:256], out[48:64, 128:256])
        return first, second

    def side_by_side(first, count):
        return jnp.concatenate([packed[(first + k) * 64 : (first + k + 1) * 64, :] for k in range(count)], axis=1)

    ones = []
    for at_x in range(4):
        for z in range(16):
            at = (at_x * 64 + z) * 16
            parts = [other_ref[y * 256 + at : y * 256 + at + 16, :].astype(F32) for y in range(4)]
            other = (parts[0] + parts[1]) + (parts[2] + parts[3])
            row = (at_x * 16 + z) * 16
            ones.append(jnp.where(from_own, sums_ref[row : row + 16, :], other))
            put(at_x * 16 + z, ones[-1])
    for at_x in range(4):
        twos = []
        for quad in range(4):
            node = at_x * 16 + quad * 4
            twos.extend(raise_four(ones[node : node + 4], packed[node * 64 : node * 64 + 256, :]))
        for k in range(8):
            put(64 + at_x * 8 + k, twos[k])
        threes = []
        for quad in range(2):
            row = (64 + at_x * 8 + quad * 4) * 64
            threes.extend(raise_four(twos[quad * 4 : quad * 4 + 4], packed[row : row + 256, :]))
        for k in range(4):
            put(96 + at_x * 4 + k, threes[k])
        row = (96 + at_x * 4) * 64
        fours = raise_four(threes, packed[row : row + 256, :])
        for k in range(2):
            put(112 + at_x * 2 + k, fours[k])

    blocks = []
    for slot in range(16):
        c = flist_ref[0, slot]
        c_y, c_core = c & 3, (c >> 2) & 1
        place = pl.multiple_of((((c >> 7) * 4 + c_y) * 16 + ((c >> 3) & 15)) * 16, 16)
        block = jnp.where(c_core == my_core, own_ref[pl.ds(place, 16), :], other_ref[pl.ds(place, 16), :])
        live = jnp.where(slot < fcount_ref[0], 1 - c_core, 2)
        blocks.append(block * jnp.where(half16 == live, 1.0, 0.0).astype(BF16))
    far = dot(jnp.concatenate(blocks, axis=1), side_by_side(112, 16), NT)

    parts = []
    for level, offset in enumerate((0, 64, 96, 112)):
        blocks = []
        for slot in range(8):
            node = tlist_ref[0, level, slot]
            block = nodes[offset + (node >> 1)]
            mask = jnp.where(half16 == (node & 1), 1.0, 0.0).astype(BF16)
            blocks.append(block * jnp.concatenate([mask, mask], axis=0))
        out = dot(jnp.concatenate(blocks, axis=1), side_by_side(128 + level * 8, 8), NT)
        parts.append(out[:16] + out[16:])
    upper = jnp.concatenate([parts[1], parts[2]], axis=1)
    last = jnp.concatenate([parts[3], parts[0]], axis=1)
    far = jnp.concatenate([far, far], axis=1)
    packed_shares = jnp.concatenate([upper, last, far], axis=0).astype(BF16)
    for k in range(8):
        shares_ref[k] = packed_shares


def mid_pass(dev, flist, fcount, tlist, own, other, sums, packed):
    return pl.pallas_call(
        mid_kernel,
        out_shape=jax.ShapeDtypeStruct((8, 48, 128), BF16),
        in_specs=smem(4) + vmem(4),
        out_specs=vmem(1)[0],
        scratch_shapes=[pltpu.VMEM((120, 32, 128), BF16)],
        compiler_params=pltpu.CompilerParams(vmem_limit_bytes=GRANT - 16 * 1024 * 1024),
        cost_estimate=pl.CostEstimate(flops=300_000_000, bytes_accessed=5_000_000, transcendentals=0),
        name="mid_pass",
    )(dev, flist, fcount, tlist, own, other, sums, packed)


def down_kernel(
    id_ref, shares_hbm, path_hbm, dt_hbm, lt_hbm, basis_hbm, near_a_hbm, near_b_hbm,
    out_ref, shares_ref, path_ref, dt_ref, lt_ref, basis_ref, near_a, near_b, sems,
):
    moves = copies(
        (shares_hbm, path_hbm, dt_hbm, lt_hbm, basis_hbm, near_a_hbm, near_b_hbm),
        (shares_ref, path_ref, dt_ref, lt_ref, basis_ref, near_a, near_b),
        sems,
    )
    for move in moves:
        move.start()
    for move in moves[:3]:
        move.wait()
    zl = (id_ref[0] >> 3) & 3
    mine = shares_ref[(id_ref[0] >> 2) & 7].astype(F32)
    upper = jnp.zeros((16, 128), F32)
    down = jnp.zeros((16, 64), F32)
    low = lax.broadcasted_iota(jnp.int32, (16, 128), 1) < 64
    for o in range(8):
        pair = jnp.where((o >> 1) == zl, 1.0, 0.0)
        quad = jnp.where((o >> 2) == (zl >> 1), 1.0, 0.0)
        share = shares_ref[o].astype(F32)
        upper = upper + share[0:16, :] * jnp.where(low, pair, quad)
        down = down + share[16:32, 0:64]
    down = upper[:, 64:128] + wide_dot(down, path_ref[2], NN)
    down = upper[:, 0:64] + wide_dot(down, path_ref[1], NN)
    down = mine[16:32, 64:128] + wide_dot(down, path_ref[0], NN)
    down = mine[32:48, 0:64] + wide_dot(down, dt_ref[0], NN)
    for move in moves[3:]:
        move.wait()
    near_refs = (near_a, near_b)
    near_blocks = [(ref, k) for ref in near_refs for k in range(ref.shape[1] // 256)]
    for leaf in range(16):
        near_ref, k = near_blocks[leaf]
        leaf_down = wide_dot(down, lt_ref[leaf], NN).astype(BF16)
        cols = slice(leaf * 256, (leaf + 1) * 256)
        near = near_ref[:, k * 256 : (k + 1) * 256]
        out_ref[:, cols] = near + dot(leaf_down, basis_ref[leaf], NN)


def down_pass(dev, shares, path, dt, lt, basis, near):
    return pl.pallas_call(
        down_kernel,
        out_shape=jax.ShapeDtypeStruct((16, 4096), F32),
        in_specs=smem(1) + hbm(7),
        out_specs=vmem(1)[0],
        scratch_shapes=[
            pltpu.VMEM((8, 48, 128), BF16),
            pltpu.VMEM((3, 64, 64), BF16),
            pltpu.VMEM((1, 64, 64), BF16),
            pltpu.VMEM((16, 64, 64), BF16),
            pltpu.VMEM((16, 64, 256), BF16),
            pltpu.VMEM(near[0].shape, F32),
            pltpu.VMEM(near[1].shape, F32),
            pltpu.SemaphoreType.DMA((7,)),
        ],
        compiler_params=pltpu.CompilerParams(vmem_limit_bytes=GRANT),
        cost_estimate=pl.CostEstimate(flops=20_000_000, bytes_accessed=1_500_000, transcendentals=0),
        name="down_pass",
    )(dev, shares, path, dt, lt, basis, *near)


def cyclic(value, axis, size, by):
    return lax.ppermute(value, axis, [(i, (i + by) % size) for i in range(size)])


def spread(value, axis, size):
    rows = value.shape[0]
    same = jnp.broadcast_to(value[None], (size, rows, 128))
    return lax.all_to_all(same, axis, 0, 0, tiled=True).reshape(size * rows, 128)


def on_device(
    rhs, coords, basis, lt, dt, t1, t2, t3, far_list, far_count, far_coupling, top_list, top_coupling,
    near_list,
):
    dev = lax.axis_index(DEV).astype(jnp.int32).reshape(1)
    tie = lax.optimization_barrier
    payload, own = up_pass(dev, rhs, coords, basis, lt, dt)
    blocks = lax.all_to_all(payload, ("zh", "zl"), 0, 0, tiled=True).reshape(256, 128)
    swap_b = lax.ppermute(own, DEV, [(i, ((i + 1) ^ 1) - 1) for i in range(1, 511)] + [(0, 511), (511, 0)])
    swap_a = lax.ppermute(own, DEV, [(i, i ^ 1) for i in range(512)])
    own, t1 = tie((own, t1))
    dev_a = order_pass(dev, t1)
    blocks, swap_b, swap_a, dev_a = tie((blocks, swap_b, swap_a, dev_a))
    near_list = jnp.transpose(near_list)
    gathered = spread(blocks, ("x", "y"), 16)
    near_a, packed, path = near_and_prep(
        dev_a, near_list, swap_a, own, swap_b, t1, t2, t3, far_coupling, top_coupling, 0, 12
    )
    gathered, near_a, packed = tie((gathered, near_a, packed))
    other = cyclic(gathered, "core", 2, 1)
    sums, packed = half_pass(gathered, packed)
    shares = mid_pass(dev, far_list, far_count, top_list, gathered, other, sums, packed)
    shares, dev_b = tie((shares, dev))
    near_b = near_field(dev_b, near_list, swap_a, own, swap_b, 12, 16)
    shares = lax.all_to_all(shares, ("zl", "core"), 0, 0, tiled=True)
    return down_pass(dev, shares, path, dt, lt, basis, (near_a, near_b))


def solution(mesh):
    torus = Mesh(mesh.devices.reshape(4, 4, 4, 2, 4), DEV)
    branch = DEV[:4]
    in_specs = (
        P(None, DEV),
        P(None, DEV),
        P(DEV, None, None),
        P(DEV, None, None),
        P(DEV, None, None),
        P(),
        P(),
        P(),
        P(DEV, None),
        P(DEV),
        P(DEV, None, None, None),
        P(branch, None, None),
        P(branch, None, None, None, None),
        P(DEV, None),
    )
    return jax.shard_map(
        on_device, mesh=torus, in_specs=in_specs, out_specs=P(None, DEV), check_vma=False
    )
```
